32 devices in a mesh: dp: 8 (over y, x, core), mp: 4 (over z).
Axes of the slice: x: 2, y: 2, z: 4, core: 2. Of those that a mesh axis runs over, the one named last changes fastest.
Arguments:
- tokens: bfloat16 [8, 1024, 768], P('dp', 'mp'), may hold values from -6 to 6
- doc_starts: int32 [8, 2], P('dp'), may hold values from 0 to 1023, as said below
- query_proj: bfloat16 [768, 768], replicated, may hold values from -0.21875 to 0.21875
- key_proj: bfloat16 [768, 768], replicated, may hold values from -0.21875 to 0.21875
- value_proj: bfloat16 [768, 768], replicated, may hold values from -0.21875 to 0.21875
- query_bias: float32 [768], replicated, may hold values from -1.2 to 1.2
- key_bias: float32 [768], replicated, may hold values from -1.2 to 1.2
- value_bias: float32 [768], replicated, may hold values from -1.2 to 1.2
- output_proj: bfloat16 [768, 768], replicated, may hold values from -1.75 to 1.75
- output_bias: float32 [768], replicated, may hold values from -1.2 to 1.2
- attn_gain: float32 [768], replicated, may hold values from 0.5 to 1.5
- attn_shift: float32 [768], replicated, may hold values from -1.2 to 1.2
- up_proj: bfloat16 [768, 3072], P(None, 'mp'), may hold values from -0.21875 to 0.21875
- up_bias: float32 [3072], P('mp'), may hold values from -1.2 to 1.2
- down_proj: bfloat16 [3072, 768], P('mp'), may hold values from -0.109375 to 0.109375
- down_bias: float32 [768], replicated, may hold values from -1.2 to 1.2
- ffn_gain: float32 [768], replicated, may hold values from 0.5 to 1.5
- ffn_shift: float32 [768], replicated, may hold values from -1.2 to 1.2
- cotangent: bfloat16 [8, 1024, 768], P('dp', 'mp'), may hold values from -6 to 6
Outputs:
- layer_out: bfloat16 [8, 1024, 768], P('dp', 'mp')
- input_grad: bfloat16 [8, 1024, 768], P('dp', 'mp')
- query_proj_grad: float32 [768, 768], replicated
- key_proj_grad: float32 [768, 768], replicated
- value_proj_grad: float32 [768, 768], replicated
- query_bias_grad: float32 [768], replicated
- key_bias_grad: float32 [768], replicated
- value_bias_grad: float32 [768], replicated
- output_proj_grad: float32 [768, 768], replicated
- output_bias_grad: float32 [768], replicated
- attn_gain_grad: float32 [768], replicated
- attn_shift_grad: float32 [768], replicated
- up_proj_grad: float32 [768, 3072], P(None, 'mp')
- up_bias_grad: float32 [3072], P('mp')
- down_proj_grad: float32 [3072, 768], P('mp')
- down_bias_grad: float32 [768], replicated
- ffn_gain_grad: float32 [768], replicated
- ffn_shift_grad: float32 [768], replicated
The draws below stay inside these ranges and needn't reach their ends.
Inputs may be any that keep to these rules, and one draw needn't show every extreme that they name: doc_starts[r, 0] = 0 and for d >= 1 doc_starts[r, d] lies in [d * 512 + 1, (d + 1) * 512); document d of row r runs from its start to the next start (or 1024) minus one.
All inputs are finite; a program needn't handle non-finite values.
Results may differ from the reference program's by a relative error of at most 0.025.
Values may be sent and summed in bfloat16 or wider, within the bound.
A program may use at most 256 MiB of HBM per device.

```python
import math
import jax
import jax.numpy as jnp
from jax import lax

D = 768
HEADS = 12
HD = 64
FF = 3072
SEQ = 1024
BLOCK = 64
DOCS = 2
ROWS = 8
SPAN = 512


def draw_doc_starts(key, part):
    offsets = jax.random.randint(key, (ROWS, DOCS), 1, SPAN)
    blocks = jnp.arange(DOCS, dtype=jnp.int32)
    row_index = jnp.arange(ROWS, dtype=jnp.int32)
    forced = (row_index[:, None] == 0) & (blocks[None, :] == DOCS - 1)
    offsets = jnp.where(forced, SPAN - 1, offsets)
    starts = blocks[None, :] * SPAN + offsets
    return jnp.where(blocks[None, :] == 0, 0, starts).astype(jnp.int32)


def block_scale(rng, shape, cuts, smallest, top_value):
    def one(dim, blocks):
        heights = jax.random.uniform(jax.random.fold_in(jax.random.fold_in(rng, 6), dim), (blocks,), jnp.float32, smallest / len(cuts), top_value / len(cuts))
        return jnp.repeat(jnp.exp(heights), shape[dim] // blocks).reshape((-1,) + (1,) * (len(shape) - dim - 1))

    level = one(*cuts[0])
    for cut in cuts[1:]:
        level = level * one(*cut)
    return level


def centred(rng, dims, deviation, most, pieces=(), held_as=jnp.bfloat16):
    drawn = deviation * jax.random.normal(rng, dims, jnp.float32)
    if pieces:
        drawn = drawn * block_scale(rng, dims, pieces, -0.22, 0.18)
    return jnp.clip(drawn, -most, most).astype(held_as)


def setup_inputs(seed: int = 0) -> dict:
    streams_of = jax.random.split(jax.random.key(seed), 20)
    return {
        "tokens": centred(streams_of[0], (ROWS, SEQ, D), 1.0, 6.0, ((0, 8), (1, 4))),
        "doc_starts": draw_doc_starts(jax.random.fold_in(streams_of[19], 71), 0),
        "query_proj": centred(streams_of[2], (D, D), D ** -0.5, 0.21875),
        "key_proj": centred(streams_of[3], (D, D), D ** -0.5, 0.21875),
        "value_proj": centred(streams_of[4], (D, D), D ** -0.5, 0.21875),
        "query_bias": centred(streams_of[5], (D,), 0.3, 1.2, (), jnp.float32),
        "key_bias": centred(streams_of[6], (D,), 0.3, 1.2, (), jnp.float32),
        "value_bias": centred(streams_of[7], (D,), 0.3, 1.2, (), jnp.float32),
        "output_proj": centred(streams_of[8], (D, D), (D // 64) ** -0.5, 1.75),
        "output_bias": centred(streams_of[9], (D,), 0.3, 1.2, (), jnp.float32),
        "attn_gain": jnp.clip(1.0 + 0.1 * jax.random.normal(streams_of[10], (D,), jnp.float32), 0.5, 1.5),
        "attn_shift": centred(streams_of[11], (D,), 0.3, 1.2, (), jnp.float32),
        "up_proj": centred(streams_of[12], (D, FF), D ** -0.5, 0.21875, ((1, 4),)),
        "up_bias": centred(streams_of[13], (FF,), 0.3, 1.2, ((0, 4),), jnp.float32),
        "down_proj": centred(streams_of[14], (FF, D), FF ** -0.5, 0.109375, ((0, 4),)),
        "down_bias": centred(streams_of[15], (D,), 0.3, 1.2, (), jnp.float32),
        "ffn_gain": jnp.clip(1.0 + 0.1 * jax.random.normal(streams_of[16], (D,), jnp.float32), 0.5, 1.5),
        "ffn_shift": centred(streams_of[17], (D,), 0.3, 1.2, (), jnp.float32),
        "cotangent": centred(streams_of[18], (ROWS, SEQ, D), 1.0, 6.0, ((0, 8), (1, 4))),
    }


@jax.custom_vjp
def low(v):
    return lax.optimization_barrier(v.astype(jnp.bfloat16)).astype(jnp.float32)

@jax.custom_vjp
def low_back(v):
    return v

def low_keep(v):
    return (low(v), None)

def low_pass(kept, grad):
    return (grad,)

def back_keep(v):
    return (v, None)

def back_low(kept, grad):
    return (low(grad),)
low.defvjp(low_keep, low_pass)
low_back.defvjp(back_keep, back_low)
highest = lax.Precision.HIGHEST

def matmul(left, right):
    return jnp.dot(left, right, precision=highest)

def layer_norm(inputs, norm_gain, norm_shift):
    center = inputs - lax.optimization_barrier(jnp.mean(inputs, axis=-1, keepdims=True))
    spread = lax.optimization_barrier(jnp.mean(center * center, axis=-1, keepdims=True))
    return center * lax.rsqrt(spread + 1e-05) * norm_gain + norm_shift

def doc_layout(starts):
    places = jnp.arange(SEQ, dtype=jnp.int32)
    inside = (starts[None, :] <= places[:, None]).astype(jnp.int32)
    number = (lax.optimization_barrier(jnp.sum(inside, axis=1)) - 1).astype(jnp.int32)
    picked = jnp.arange(DOCS, dtype=jnp.int32)[None, :] == number[:, None]
    ending = jnp.concatenate([starts[1:], jnp.full((1,), SEQ, jnp.int32)])
    opened = lax.optimization_barrier(jnp.sum(jnp.where(picked, starts[None, :], 0), axis=1)).astype(jnp.int32)
    closed = lax.optimization_barrier(jnp.sum(jnp.where(picked, ending[None, :], 0), axis=1)).astype(jnp.int32)
    angles = (places - opened).astype(jnp.float32) * (0.5 * math.pi) / (closed - opened).astype(jnp.float32)
    return (number, jnp.cos(angles), jnp.sin(angles))

def features(pre_act, cos_part, sin_part):
    head_vals = jax.nn.relu(pre_act).reshape(SEQ, HEADS, HD)
    combined = jnp.concatenate([head_vals * cos_part[:, None, None], head_vals * sin_part[:, None, None]], axis=2)
    return low(combined).reshape(SEQ // BLOCK, BLOCK, HEADS, 2 * HD)

def linear_attention(query_in, key_in, value_in, number, cos_part, sin_part):
    block_count = SEQ // BLOCK
    query_feats = features(query_in, cos_part, sin_part)
    key_feats = features(key_in, cos_part, sin_part)
    values = low(value_in).reshape(block_count, BLOCK, HEADS, HD)
    doc_ids = number.reshape(block_count, BLOCK)
    within = jnp.arange(BLOCK, dtype=jnp.int32)
    allowed = (within[:, None] >= within[None, :])[None] & (doc_ids[:, :, None] == doc_ids[:, None, :])
    scores = jnp.einsum('nihf,njhf->nhij', query_feats, key_feats, precision=highest)
    scores = low_back(jnp.where(allowed[:, None], scores, 0.0))
    local_part = jnp.einsum('nhij,njhd->nihd', low(scores), values, precision=highest)
    score_sums = lax.optimization_barrier(jnp.sum(scores, axis=3)).transpose(0, 2, 1)
    lastdoc = doc_ids[:, -1]
    in_last = (doc_ids == lastdoc[:, None]).astype(jnp.float32)
    contrib = low_back(jnp.einsum('njhf,njhd->nhfd', key_feats * in_last[:, :, None, None], values, precision=highest))
    key_sums = jnp.einsum('njhf,nj->nhf', key_feats, in_last, precision=highest)
    block_ids = jnp.arange(block_count, dtype=jnp.int32)
    linked = ((block_ids[None, :] <= block_ids[:, None]) & (lastdoc[None, :] == lastdoc[:, None])).astype(jnp.float32)
    states = jnp.einsum('cb,bhfd->chfd', linked, contrib, precision=highest)
    state_sums = jnp.einsum('cb,bhf->chf', linked, key_sums, precision=highest)
    prior_states = jnp.concatenate([jnp.zeros_like(states[:1]), states[:-1]])
    prior_sums = jnp.concatenate([jnp.zeros_like(state_sums[:1]), state_sums[:-1]])
    prevdoc = jnp.concatenate([jnp.full((1,), -1, jnp.int32), lastdoc[:-1]])
    carried = (doc_ids == prevdoc[:, None]).astype(jnp.float32)
    remote = jnp.einsum('nihf,nhfd->nihd', query_feats, low(prior_states), precision=highest) * carried[:, :, None, None]
    remote_den = jnp.einsum('nihf,nhf->nih', query_feats, prior_sums, precision=highest) * carried[:, :, None]
    numerator = low_back(local_part + remote)
    denominator = jnp.maximum(score_sums + remote_den, 1.0)
    context = low(low_back(numerator / denominator[..., None]))
    return context.reshape(SEQ, HEADS * HD)

def layer_row(row_vals, starts, params):
    query_proj, key_proj, value_proj, query_bias, key_bias, value_bias, output_proj, output_bias, attn_gain, attn_shift, up_proj, up_bias, down_proj, down_bias, ffn_gain, ffn_shift = params
    number, cos_part, sin_part = doc_layout(starts)
    query_in = low_back(matmul(row_vals, query_proj)) + query_bias
    key_in = low_back(matmul(row_vals, key_proj)) + key_bias
    value_in = low_back(matmul(row_vals, value_proj)) + value_bias
    context = linear_attention(query_in, key_in, value_in, number, cos_part, sin_part)
    hidden = row_vals + low_back(matmul(context, output_proj)) + output_bias
    normed = layer_norm(hidden, attn_gain, attn_shift)
    upper = low_back(matmul(low(normed), up_proj)) + up_bias
    acted = low(jax.nn.gelu(upper, approximate=True))
    merged = normed + low_back(matmul(acted, down_proj)) + down_bias
    return layer_norm(merged, ffn_gain, ffn_shift)

def reference(tokens, doc_starts, query_proj, key_proj, value_proj, query_bias, key_bias, value_bias, output_proj, output_bias, attn_gain, attn_shift, up_proj, up_bias, down_proj, down_bias, ffn_gain, ffn_shift, cotangent):
    params = tuple((weight.astype(jnp.float32) for weight in (query_proj, key_proj, value_proj, query_bias, key_bias, value_bias, output_proj, output_bias, attn_gain, attn_shift, up_proj, up_bias, down_proj, down_bias, ffn_gain, ffn_shift)))
    token_vals = tokens.astype(jnp.float32)

    def forward(inputs, weights):

        def row_step(state_in, row_item):
            row_vals, row_starts = row_item
            return (state_in, layer_row(row_vals, row_starts, weights))
        unused, outputs = lax.scan(jax.checkpoint(row_step), jnp.zeros((), jnp.float32), (inputs, doc_starts))
        return outputs
    result, pullback = jax.vjp(forward, token_vals, params)
    input_grad, param_grads = pullback(cotangent.astype(jnp.float32))
    g_query, g_key, g_value, g_qbias, g_kbias, g_vbias, g_output, g_obias, g_again, g_ashift, g_up, g_ubias, g_down, g_dbias, g_fgain, g_fshift = param_grads
    return (result.astype(jnp.bfloat16), input_grad.astype(jnp.bfloat16), g_query, g_key, g_value, g_qbias, g_kbias, g_vbias, g_output, g_obias, g_again, g_ashift, g_up, g_ubias, g_down, g_dbias, g_fgain, g_fshift)
```

```python
import math

import jax
import jax.numpy as jnp
from jax import lax
from jax.experimental import pallas as pl
from jax.experimental.pallas import tpu as pltpu
from jax.sharding import PartitionSpec as P

HEADS = 12
HD = 64
SEQ = 1024
DOCS = 2
PAIR = 2 * HD
PAIRS = HEADS // 2
TILE = 256
MESH = pl.DeviceIdType.MESH
BF = jnp.bfloat16
F32 = jnp.float32
C0 = math.sqrt(2.0 / math.pi)
C1 = 0.044715


def mm(a, b):
    return lax.dot_general(a, b, (((1,), (0,)), ((), ())), preferred_element_type=F32)


def mm_nt(a, b):
    return lax.dot_general(a, b, (((1,), (1,)), ((), ())), preferred_element_type=F32)


def mm_tn(a, b):
    return lax.dot_general(a, b, (((0,), (0,)), ((), ())), preferred_element_type=F32)


def gelu_both(u):
    square = u * u
    t = jnp.tanh(C0 * u * (1.0 + C1 * square))
    half = 0.5 * (1.0 + t)
    slope = half + (0.5 * C0) * u * (1.0 - t * t) * (1.0 + (3.0 * C1) * square)
    return u * half, slope


def two_parts(x):
    high = x.astype(BF)
    return jnp.concatenate([high, (x - high.astype(F32)).astype(BF)], axis=1)


def col_sum(x):
    return jnp.sum(x, axis=0, keepdims=True)


def build(dp_size, mp_size, rows, width, shard):
    nbits = dp_size.bit_length() - 1
    nhalf = min(3, nbits)
    slices = 1 << nhalf
    piece = width >> nhalf
    ALL = pl.ds(0, rows)

    def order(kind):
        first = list(range(nhalf))
        if kind == 1 and nhalf == 3:
            first = [0, 2, 1]
        return first

    def w_order(kind):
        plain = order(kind)
        return plain[1:] + plain[:1]

    jobs = [order(0), order(1), order(0), order(1), order(0), order(1)]

    def kernel(
        starts, tok, cot, wq, wk, wv, wo, vec, up_hbm, down_hbm,
        out_layer, out_input, out_attn, out_ff, out_small,
        wu, wd, ub, rq, rk, vv, m2, mt2, cols, o2, bb, c1, ec, masks,
        state, state_in, ssum, ssum_in, grad_in, gsum_in, state_out, ssum_out, grad_out, gsum_out,
        num, den, ctx, hid, rstd, normed, nf, mf, acted, gps, acc, mg, ulow, hlow, cg, ngr, dgr,
        gq, gk, gv, part, gsum, red0, red1, red2, redx, zr, small, smallr, smallz, tokt, in_out,
        local_sem, send_sem, recv_sem,
    ):
        dp = lax.axis_index("dp")
        mp = lax.axis_index("mp")
        counter = [0]
        locals_used = [0]

        def bit(b):
            return lax.rem(lax.div(dp, 1 << b), 2)

        def flip(b):
            return {"dp": dp + (1 - 2 * bit(b)) * (1 << b)}

        def peer(r):
            return {"mp": lax.rem(mp + r, mp_size)}

        def remote(src, dst, device):
            i = counter[0]
            counter[0] += 1
            return pltpu.make_async_remote_copy(
                src_ref=src, dst_ref=dst, send_sem=send_sem.at[i], recv_sem=recv_sem.at[i],
                device_id=device, device_id_type=MESH,
            )

        def local(src, dst):
            i = locals_used[0]
            locals_used[0] += 1
            return pltpu.make_async_copy(src, dst, local_sem.at[i])

        def rds(start, size, unit=16):
            return pl.ds(pl.multiple_of(start, unit), size)

        barrier = pltpu.get_barrier_semaphore()
        for b in range(nbits):
            pl.semaphore_signal(barrier, inc=1, device_id=flip(b), device_id_type=MESH)
        for r in range(1, mp_size):
            pl.semaphore_signal(barrier, inc=1, device_id=peer(r), device_id_type=MESH)
        own_up = local(up_hbm, wu.at[mp])
        own_down = local(down_hbm, wd.at[mp])
        own_up.start()
        own_down.start()
        ub[mp] = jnp.broadcast_to(vec[15:16, :], (8, shard))
        own_up.wait()
        own_down.wait()
        pl.semaphore_wait(barrier, nbits + mp_size - 1)

        def w_base(kind, upto):
            bits = w_order(kind)
            base = 0
            for s in range(nhalf - 1, upto - 1, -1):
                base = base + bit(bits[s]) * (piece << s)
            return base

        w_stages = []
        stage = []
        for kind, buf in ((0, wu), (1, wd)):
            base = w_base(kind, 0)
            for r in range(1, mp_size):
                ref = buf.at[mp, rds(base, piece)]
                stage.append(remote(ref, ref, peer(r)))
        for r in range(1, mp_size):
            stage.append(remote(ub.at[mp], ub.at[mp], peer(r)))
        w_stages.append(stage)
        for s in range(nhalf):
            stage = []
            for kind, buf in ((0, wu), (1, wd)):
                base = w_base(kind, s)
                for r in range(1, mp_size):
                    t = lax.rem(mp + r, mp_size)
                    ref = buf.at[t, rds(base, piece << s)]
                    stage.append(remote(ref, ref, flip(w_order(kind)[s])))
            w_stages.append(stage)

        def weights_step(s):
            if s > 0:
                for copy in w_stages[s - 1]:
                    copy.wait()
            if s < len(w_stages):
                for copy in w_stages[s]:
                    copy.start()

        weights_step(0)

        own_start = mp * rows

        def layout(places):
            opened = jnp.full(places.shape, 0, jnp.int32) + starts[0, 0]
            closed = jnp.full(places.shape, SEQ, jnp.int32)
            if DOCS > 1:
                closed = jnp.full(places.shape, 0, jnp.int32) + starts[0, 1]
            number = jnp.zeros(places.shape, jnp.int32)
            for d in range(1, DOCS):
                ending = starts[0, d + 1] if d + 1 < DOCS else SEQ
                inside = places >= starts[0, d]
                opened = jnp.where(inside, starts[0, d], opened)
                closed = jnp.where(inside, ending, closed)
                number = number + inside.astype(jnp.int32)
            angles = (places - opened).astype(F32) * (0.5 * math.pi) / (closed - opened).astype(F32)
            return number, jnp.cos(angles), jnp.sin(angles)

        places = own_start + lax.broadcasted_iota(jnp.int32, (rows, 128), 0)
        number_c, cos_c, sin_c = layout(places)
        row_places = own_start + lax.broadcasted_iota(jnp.int32, (8, rows), 1)
        number_r, cos_r, sin_r = layout(row_places)
        edge = jnp.zeros((8, 128), jnp.int32)
        last, _, _ = layout(edge + own_start + (rows - 1))
        before, _, _ = layout(edge + own_start - 1)
        has_prev = jnp.where(edge + mp > 0, 1.0, 0.0)
        carried = jnp.where(number_c == before[:1], 1.0, 0.0) * has_prev[:1]
        in_last = jnp.where(number_c == last[:1], 1.0, 0.0)
        linked = (jnp.where(before == last, 1.0, 0.0) * has_prev)[:1]
        cols[0] = cos_c * carried
        cols[1] = sin_c * carried
        cols[2] = cos_c * in_last
        cols[3] = sin_c * in_last
        linked2 = jnp.concatenate([linked, linked], axis=1)
        linked6 = jnp.concatenate([linked] * (width // 128), axis=1)
        wide = jnp.concatenate([number_c, number_c], axis=1)
        wide_cos = jnp.concatenate([cos_c, cos_c], axis=1)
        wide_sin = jnp.concatenate([sin_c, sin_c], axis=1)
        row_id = lax.broadcasted_iota(jnp.int32, (rows, rows), 0)
        col_id = lax.broadcasted_iota(jnp.int32, (rows, rows), 1)
        angle_gap = wide_cos * cos_r[:1] + wide_sin * sin_r[:1]
        same = wide == number_r[:1]
        lower = jnp.where(same & (col_id <= row_id), angle_gap, 0.0)
        upper_part = jnp.where(same & (col_id >= row_id), angle_gap, 0.0)
        m2[:, :rows] = lower
        m2[:, rows:] = lower
        mt2[:, :rows] = upper_part
        mt2[:, rows:] = upper_part

        lane = lax.broadcasted_iota(jnp.int32, (rows, PAIR), 1)
        low_f = jnp.where(lane < HD, 1.0, 0.0)
        high_f = 1.0 - low_f
        first_two = jnp.where(lax.rem(lane, HD) < 2, 1.0, 0.0)
        o2[:rows, :] = low_f.astype(BF)
        o2[rows:, :] = high_f.astype(BF)
        c1[:rows, :] = (first_two * low_f).astype(BF)
        c1[rows:, :] = (first_two * high_f).astype(BF)
        ec[...] = first_two.astype(BF)
        block_row = lax.broadcasted_iota(jnp.int32, (2 * PAIR, PAIR), 0)
        block_col = lax.broadcasted_iota(jnp.int32, (2 * PAIR, PAIR), 1)
        bb[...] = jnp.where(
            lax.div(lax.rem(block_row, PAIR), HD) == lax.div(block_col, HD), 1.0, 0.0
        ).astype(BF)
        lo = low_f.astype(BF)[:16]
        hi = high_f.astype(BF)[:16]
        masks[0] = lo
        masks[1] = hi
        masks[2] = jnp.where(lax.rem(lane, HD) == 0, 1.0, 0.0).astype(BF)[:16]
        masks[3] = jnp.where(lax.rem(lane, HD) == 1, 1.0, 0.0).astype(BF)[:16]

        def halves(x):
            return jnp.concatenate([x * masks[0, :1], x * masks[1, :1]], axis=0)

        def expand(compact):
            low4 = jnp.concatenate([masks[0, :1]] * 2, axis=1)
            high4 = jnp.concatenate([masks[1, :1]] * 2, axis=1)
            return jnp.concatenate([compact * low4, compact * high4], axis=0)

        def compact_of(full):
            low4 = jnp.concatenate([masks[0, :1]] * 2, axis=1).astype(F32)
            high4 = jnp.concatenate([masks[1, :1]] * 2, axis=1).astype(F32)
            return full[:HD] * low4 + full[HD:] * high4

        for index, (weight, out) in enumerate(((wq, rq), (wk, rk), (wv, vv))):
            for j in range(width // TILE):
                at = pl.ds(j * TILE, TILE)
                y = mm(tok[...], weight[:, at]) + vec[index : index + 1, at]
                if index < 2:
                    y = jnp.maximum(y, 0.0)
                out[:, at] = y.astype(BF)

        def lanes(p):
            return pl.ds(pl.multiple_of(p * PAIR, PAIR), PAIR)

        def feats(ref, p, which):
            x = ref[:, lanes(p)].astype(F32)
            return (x * cols[which]).astype(BF), (x * cols[which + 1]).astype(BF)

        def contribs(p, carry):
            kc, ks = feats(rk, p, 2)
            full = mm_tn(vv[:, lanes(p)], jnp.concatenate([kc, ks], axis=1))
            state[p] = compact_of(full)
            ssum[0:1, lanes(p)] = col_sum(kc.astype(F32))
            ssum[1:2, lanes(p)] = col_sum(ks.astype(F32))
            return carry

        ssum[...] = jnp.zeros_like(ssum)
        lax.fori_loop(0, PAIRS, contribs, 0)

        def local_attention(p, carry):
            k2 = halves(rk[:, lanes(p)])
            a = (mm_nt(rq[:, lanes(p)], k2) * m2[...]).astype(BF)
            both = mm(a, jnp.concatenate([halves(vv[:, lanes(p)]), o2[...]], axis=1))
            num[:, lanes(p)] = both[:, :PAIR]
            den[:, lanes(p)] = both[:, PAIR:]
            return carry

        def chain(out_state, out_sum, in_state, in_sum, source, source_sum, forward):
            step = 1 if forward else mp_size - 1
            has_in = (mp > 0) if forward else (mp < mp_size - 1)
            has_out = (mp < mp_size - 1) if forward else (mp > 0)
            copies = [
                remote(out_state, in_state, peer(step)),
                remote(out_sum, in_sum, peer(step)),
            ]

            @pl.when(jnp.logical_not(has_in))
            def _():
                in_state[...] = jnp.zeros_like(in_state)
                in_sum[...] = jnp.zeros_like(in_sum)

            @pl.when(has_in)
            def _():
                for copy in copies:
                    copy.wait_recv()

            def fill(p, carry):
                value = source[p] + in_state[p].astype(F32) * linked2
                out_state[p] = value.astype(BF)
                return carry

            lax.fori_loop(0, PAIRS, fill, 0)
            out_sum[...] = source_sum[...] + in_sum[...] * linked6

            @pl.when(has_out)
            def _():
                for copy in copies:
                    copy.start()

            def finish():
                @pl.when(has_out)
                def _():
                    for copy in copies:
                        copy.wait_send()

            return finish

        lax.fori_loop(0, PAIRS, local_attention, 0)
        finish_forward = chain(state_out, ssum_out, state_in, ssum_in, state, ssum, True)
        weights_step(1)

        def remote_attention(p, carry):
            at = lanes(p)
            qc, qs = feats(rq, p, 0)
            carry_num = mm_nt(jnp.concatenate([qc, qs], axis=1), expand(state_in[p]))
            weighted = qc.astype(F32) * ssum_in[0:1, at] + qs.astype(F32) * ssum_in[1:2, at]
            total = den[:, at] + mm(two_parts(weighted), bb[...])
            value = (num[:, at] + carry_num) / jnp.maximum(total, 1.0)
            den[:, at] = total
            num[:, at] = value
            ctx[:, at] = value.astype(BF)
            return carry

        lax.fori_loop(0, PAIRS, remote_attention, 0)

        for j in range(width // TILE):
            at = pl.ds(j * TILE, TILE)
            hid[:, at] = tok[:, at].astype(F32) + mm(ctx[...], wo[:, at]) + vec[3:4, at]
        weights_step(2)
        RB = 64

        def first_norm(i, carry):
            at = pl.ds(pl.multiple_of(i * RB, RB), RB)
            x = hid[at, :]
            center = x - jnp.mean(x, axis=1, keepdims=True)
            inv = lax.rsqrt(jnp.mean(center * center, axis=1, keepdims=True) + 1e-05)
            xhat = center * inv
            y = xhat * vec[4:5, :] + vec[5:6, :]
            hid[at, :] = xhat
            rstd[at, :] = jnp.broadcast_to(inv, (RB, 128))
            normed[at, :] = y
            nf[mp, at, :] = y.astype(BF)
            return carry

        lax.fori_loop(0, rows // RB, first_norm, 0)
        norm_copies = [remote(nf.at[mp], nf.at[mp], peer(r)) for r in range(1, mp_size)]
        for copy in norm_copies:
            copy.start()
        weights_step(3)
        weights_step(4)

        def ffn_up(r, carry):
            t = lax.rem(mp + r, mp_size)
            for j in range(shard // TILE):
                at = pl.ds(j * TILE, TILE)
                u = mm(nf[mp], wu[t, :, at]) + ub[t, 0:1, at]
                value, slope = gelu_both(u)
                acted[t, :, at] = value.astype(BF)
                gps[t, :, at] = slope
            return carry

        lax.fori_loop(0, mp_size, ffn_up, 0)
        acc[...] = jnp.zeros_like(acc)

        def ffn_down(r, carry):
            t = lax.rem(mp + r, mp_size)
            for j in range(width // TILE):
                at = pl.ds(j * TILE, TILE)
                acc[:, at] += mm(acted[t], wd[t, :, at])
            return carry

        lax.fori_loop(0, mp_size, ffn_down, 0)
        small[0] = jnp.zeros_like(small[0])

        def second_norm(i, carry):
            at = pl.ds(pl.multiple_of(i * RB, RB), RB)
            x = normed[at, :] + acc[at, :] + vec[6:7, :]
            center = x - jnp.mean(x, axis=1, keepdims=True)
            inv = lax.rsqrt(jnp.mean(center * center, axis=1, keepdims=True) + 1e-05)
            xhat = center * inv
            in_out[0, at, :] = (xhat * vec[7:8, :] + vec[8:9, :]).astype(BF)
            g = cot[at, :].astype(F32)
            s = g * vec[7:8, :]
            grad = (
                s - jnp.mean(s, axis=1, keepdims=True) - xhat * jnp.mean(s * xhat, axis=1, keepdims=True)
            ) * inv
            mg[at, :] = grad
            mf[mp, at, :] = grad.astype(BF)
            small[0, 7:8, :] += col_sum(g * xhat)
            small[0, 8:9, :] += col_sum(g)
            small[0, 6:7, :] += col_sum(grad)
            return carry

        lax.fori_loop(0, rows // RB, second_norm, 0)
        layer_copy = local(in_out.at[0], out_layer)
        layer_copy.start()
        merged_copies = [remote(mf.at[mp], mf.at[mp], peer(r)) for r in range(1, mp_size)]
        for copy in merged_copies:
            copy.start()

        def ffn_back(r, carry):
            t = lax.rem(mp + r, mp_size)
            for j in range(shard // TILE):
                at = pl.ds(j * TILE, TILE)
                up_grad = mm_nt(mf[mp], wd[t, at, :]) * gps[t, :, at]
                ulow[:, at] = up_grad.astype(BF)
            for j in range(width // TILE):
                at = pl.ds(j * TILE, TILE)
                mg[:, at] += mm_nt(ulow[...], wu[t, at, :])
            return carry

        lax.fori_loop(0, mp_size, ffn_back, 0)

        def norm_back(i, carry):
            at = pl.ds(pl.multiple_of(i * RB, RB), RB)
            g = mg[at, :]
            xhat = hid[at, :]
            s = g * vec[4:5, :]
            inv = rstd[at, 0:1]
            grad = (
                s - jnp.mean(s, axis=1, keepdims=True) - xhat * jnp.mean(s * xhat, axis=1, keepdims=True)
            ) * inv
            acc[at, :] = grad
            hlow[at, :] = grad.astype(BF)
            small[0, 4:5, :] += col_sum(g * xhat)
            small[0, 5:6, :] += col_sum(g)
            small[0, 3:4, :] += col_sum(grad)
            return carry

        lax.fori_loop(0, rows // RB, norm_back, 0)
        for j in range(width // TILE):
            at = pl.ds(j * TILE, TILE)
            cg[:, at] = mm_nt(hlow[...], wo[at, :]).astype(BF)

        def back_state(p, carry):
            at = lanes(p)
            total = den[:, at]
            inv = 1.0 / jnp.maximum(total, 1.0)
            g = cg[:, at].astype(F32)
            numer = (g * inv).astype(BF)
            sums = mm(two_parts(g * num[:, at]), bb[...])
            den_grad = jnp.where(total > 1.0, -sums * inv, 0.0)
            ngr[:, at] = numer
            dgr[:, at] = den_grad
            qc, qs = feats(rq, p, 0)
            full = mm_tn(numer, jnp.concatenate([qc, qs], axis=1))
            state[p] = compact_of(full)
            ssum[0:1, at] = col_sum(qc.astype(F32) * den_grad)
            ssum[1:2, at] = col_sum(qs.astype(F32) * den_grad)
            return carry

        lax.fori_loop(0, PAIRS, back_state, 0)
        finish_forward()

        def back_local(p, carry):
            at = lanes(p)
            qp = rq[:, at]
            kp = rk[:, at]
            vp = vv[:, at]
            numer = ngr[:, at]
            den_grad = dgr[:, at]
            k2 = halves(kp)
            q2 = halves(qp)
            n2 = halves(numer)
            dh = den_grad.astype(BF)
            dl = (den_grad - dh.astype(F32)).astype(BF)
            x = dh * masks[2, :1] + dl * masks[3, :1]
            ds = (
                mm_nt(
                    jnp.concatenate([numer, x], axis=1),
                    jnp.concatenate([halves(vp), c1[...]], axis=1),
                )
                * m2[...]
            ).astype(BF)
            grad_q = mm(ds, k2)
            at_scores = (mm_nt(kp, q2) * mt2[...]).astype(BF)
            gv_part = mm(at_scores, n2)
            dst = (
                mm_nt(
                    jnp.concatenate([vp, ec[...]], axis=1),
                    jnp.concatenate([n2, halves(x)], axis=1),
                )
                * mt2[...]
            ).astype(BF)
            gk_part = mm(dst, q2)
            t = mm(numer, expand(state_in[p]))
            cq = cols[0]
            sq = cols[1]
            grad_q = grad_q + cq * t[:, :PAIR] + sq * t[:, PAIR:]
            grad_q = grad_q + den_grad * (cq * ssum_in[0:1, at] + sq * ssum_in[1:2, at])
            grad_q = jnp.where(qp.astype(F32) > 0.0, grad_q, 0.0)
            small[0, 0:1, at] = col_sum(grad_q)
            gq[:, at] = grad_q.astype(BF)
            normed[:, at] = gk_part
            hid[:, at] = gv_part
            return carry

        lax.fori_loop(0, PAIRS, back_local, 0)
        finish_backward = chain(grad_out, gsum_out, grad_in, gsum_in, state, ssum, False)

        tokt[...] = tok[...].T

        def weight_grad(index, left_t, right):
            def body(i, carry):
                at = rds(i * TILE, TILE, TILE)
                for j in range(width // TILE):
                    to = pl.ds(j * TILE, TILE)
                    part[rds(index * width + i * TILE, TILE, TILE), to] = mm(
                        left_t[at, :], right[:, to]
                    ).astype(BF)
                return carry

            lax.fori_loop(0, width // TILE, body, 0)

        weight_grad(0, tokt, gq)

        def back_remote(p, carry):
            at = lanes(p)
            full = expand(grad_in[p])
            t = mm(vv[:, at], full)
            kc, ks = feats(rk, p, 2)
            ck = cols[2]
            sk = cols[3]
            grad_k = normed[:, at] + ck * (t[:, :PAIR] + gsum_in[0:1, at]) + sk * (
                t[:, PAIR:] + gsum_in[1:2, at]
            )
            grad_k = jnp.where(rk[:, at].astype(F32) > 0.0, grad_k, 0.0)
            small[0, 1:2, at] = col_sum(grad_k)
            gk[:, at] = grad_k.astype(BF)
            grad_v = hid[:, at] + mm_nt(jnp.concatenate([kc, ks], axis=1), full)
            small[0, 2:3, at] = col_sum(grad_v)
            gv[:, at] = grad_v.astype(BF)
            return carry

        lax.fori_loop(0, PAIRS, back_remote, 0)
        weight_grad(1, tokt, gk)
        weight_grad(2, tokt, gv)
        tokt[...] = ctx[...].T
        weight_grad(3, tokt, hlow)

        def j_base(job, upto):
            base = 0
            for s in range(upto):
                base = base + bit(jobs[job][s]) * (width >> (s + 1))
            return base

        reds = [red0, red1, red2]
        rs_copies = {}

        def rs_start(job, s):
            half = width >> (s + 1)
            b = jobs[job][s]
            away = job * width + j_base(job, s) + (1 - bit(b)) * half
            copy = remote(part.at[rds(away, half)], reds[s].at[job], flip(b))
            copy.start()
            rs_copies[job, s] = copy

        def rs_finish(job, s):
            half = width >> (s + 1)
            rs_copies[job, s].wait()
            keep = job * width + j_base(job, s + 1)
            step = min(half, 96)

            def body(i, carry):
                at = rds(keep + i * step, step)
                part[at, :] = (
                    part[at, :].astype(F32) + reds[s][job, rds(i * step, step), :].astype(F32)
                ).astype(BF)
                return carry

            lax.fori_loop(0, half // step, body, 0)

        def extra(job):
            for e, b in enumerate(range(nhalf, nbits)):
                at = rds(job * width + j_base(job, nhalf), piece)
                copy = remote(part.at[at], redx.at[job, e], flip(b))
                copy.start()
                copy.wait()
                part[at, :] = (part[at, :].astype(F32) + redx[job, e].astype(F32)).astype(BF)

        def ag_copy(job, s):
            size = width >> (s + 1)
            at = rds(job * width + j_base(job, s + 1), size)
            return remote(gsum.at[at], gsum.at[at], flip(jobs[job][s]))

        def run_small():
            for b in range(nbits):
                copy = remote(small.at[b], smallr.at[b], flip(b))
                copy.start()
                copy.wait()
                small[b + 1] = small[b] + smallr[b]
            smallz[mp] = small[nbits]
            copies = [remote(smallz.at[mp], smallz.at[mp], peer(r)) for r in range(1, mp_size)]
            for copy in copies:
                copy.start()
            for copy in copies:
                copy.wait()
            total = smallz[0]
            for z in range(1, mp_size):
                total = total + smallz[z]
            smallr[0, 0:8] = total[0:8]
            keep_row = lax.broadcasted_iota(jnp.int32, (8, width), 0) == 7
            smallr[0, 8:16] = jnp.where(keep_row, small[nbits, 8:16], total[8:16])

        attn_jobs = list(range(4))
        for job in attn_jobs:
            rs_start(job, 0)

        for j in range(width // TILE):
            at = pl.ds(j * TILE, TILE)
            total = acc[:, at] + mm_nt(gq[...], wq[at, :]) + mm_nt(gk[...], wk[at, :])
            in_out[1, :, at] = (total + mm_nt(gv[...], wv[at, :])).astype(BF)
        input_copy = local(in_out.at[1], out_input)
        input_copy.start()

        for job in attn_jobs:
            rs_finish(job, 0)
            rs_start(job, 1)

        for copy in norm_copies:
            copy.wait()
        for copy in merged_copies:
            copy.wait()
        tiles = width // TILE
        gps[...] = jnp.zeros_like(gps)

        def shard_grads(c, carry):
            for j in range(shard // TILE):
                at = pl.ds(j * TILE, TILE)
                u = mm(nf[c], wu[mp, :, at]) + ub[mp, 0:1, at]
                value, slope = gelu_both(u)
                up_grad = mm_nt(mf[c], wd[mp, at, :]) * slope
                small[0, 15:16, at] += col_sum(up_grad)
                gq[:, at] = value.astype(BF)
                ulow[:, at] = up_grad.astype(BF)
            for j in range(tiles):
                at = pl.ds(j * TILE, TILE)
                gps[j] += mm_tn(nf[c, :, at], ulow[...])
                gps[tiles + j] += mm_tn(gq[:, at], mf[c])
            return carry

        lax.fori_loop(0, mp_size, shard_grads, 0)
        for index in range(2):
            for j in range(width // TILE):
                part[pl.ds((4 + index) * width + j * TILE, TILE), :] = gps[index * tiles + j].astype(BF)
        for job in (4, 5):
            rs_start(job, 0)
        for s in range(1, nhalf):
            for job in attn_jobs:
                rs_finish(job, s)
                if s + 1 < nhalf:
                    rs_start(job, s + 1)
            for job in (4, 5):
                rs_finish(job, s - 1)
                rs_start(job, s)
        for job in attn_jobs:
            extra(job)

        quarter = piece // 2

        def quarter_row(first, t):
            which = lax.div(t, 2)
            base = (1 - which) * j_base(first, nhalf) + which * j_base(first + 1, nhalf)
            return (first + which) * width + base + lax.rem(t, 2) * quarter

        z_copies = {}
        for first in (0, 2):
            z_copies[first] = []
            for r in range(1, mp_size):
                t = lax.rem(mp + r, mp_size)
                z_copies[first].append(
                    remote(part.at[rds(quarter_row(first, t), quarter)], zr.at[first // 2, r - 1], peer(r))
                )
            for copy in z_copies[first]:
                copy.start()
        for job in (4, 5):
            rs_finish(job, nhalf - 1)
            extra(job)
            at = rds(job * width + j_base(job, nhalf), piece)
            gsum[at, :] = part[at, :]
        ff_ag = [ag_copy(job, nhalf - 1) for job in (4, 5)]
        for copy in ff_ag:
            copy.start()
        z_back = {}
        for first in (0, 2):
            for copy in z_copies[first]:
                copy.wait()
            at = rds(quarter_row(first, mp), quarter)
            total = part[at, :].astype(F32)
            for r in range(mp_size - 1):
                total = total + zr[first // 2, r].astype(F32)
            gsum[at, :] = total.astype(BF)
            z_back[first] = [remote(gsum.at[at], gsum.at[at], peer(r)) for r in range(1, mp_size)]
            for copy in z_back[first]:
                copy.start()
        run_small()
        for first in (0, 2):
            for copy in z_back[first]:
                copy.wait()
        pending = {job: ff_ag[job - 4] for job in (4, 5)}
        for job in attn_jobs:
            pending[job] = ag_copy(job, nhalf - 1)
            pending[job].start()
        for s in range(nhalf - 2, -1, -1):
            for job in (4, 5, 0, 1, 2, 3):
                pending[job].wait()
                pending[job] = ag_copy(job, s)
                pending[job].start()
        for job in (4, 5, 0, 1, 2, 3):
            pending[job].wait()
        outs = [
            local(gsum.at[pl.ds(0, 4 * width)], out_attn),
            local(gsum.at[pl.ds(4 * width, 2 * width)], out_ff),
            local(smallr.at[0], out_small),
        ]
        for copy in outs:
            copy.start()
        finish_backward()
        layer_copy.wait()
        input_copy.wait()
        for copy in outs:
            copy.wait()

    def call(*operands):
        vm = pltpu.VMEM
        big = lambda *s: vm(s, BF)
        flt = lambda *s: vm(s, F32)
        nsem = 160
        scratch = [
            big(mp_size, width, shard), big(mp_size, shard, width), flt(mp_size, 8, shard),
            big(rows, width), big(rows, width), big(rows, width),
            flt(rows, 2 * rows), flt(rows, 2 * rows), flt(4, rows, 128),
            big(2 * rows, PAIR), big(2 * PAIR, PAIR), big(2 * rows, PAIR), big(rows, PAIR), big(4, 16, PAIR),
            flt(PAIRS, HD, 2 * PAIR), big(PAIRS, HD, 2 * PAIR), flt(8, width), flt(8, width),
            big(PAIRS, HD, 2 * PAIR), flt(8, width), big(PAIRS, HD, 2 * PAIR), flt(8, width),
            big(PAIRS, HD, 2 * PAIR), flt(8, width),
            flt(rows, width), flt(rows, width), big(rows, width), flt(rows, width), flt(rows, 128),
            flt(rows, width), big(mp_size, rows, width), big(mp_size, rows, width),
            big(mp_size, rows, shard), flt(2 * (width // TILE), rows, shard), flt(rows, width), flt(rows, width),
            big(rows, shard), big(rows, width), big(rows, width), big(rows, width), flt(rows, width),
            big(rows, width), big(rows, width), big(rows, width),
            big(6 * width, width), big(6 * width, width),
            big(6, width // 2, width), big(6, width // 4, width), big(6, width // 8, width),
            big(6, max(1, nbits - nhalf), piece, width), big(2, mp_size - 1, piece // 2, width),
            flt(nbits + 1, 16, width), flt(nbits, 16, width), flt(mp_size, 16, width),
            big(width, rows), big(2, rows, width),
            pltpu.SemaphoreType.DMA((16,)), pltpu.SemaphoreType.DMA((nsem,)), pltpu.SemaphoreType.DMA((nsem,)),
        ]
        spec = pl.BlockSpec(memory_space=pltpu.VMEM)
        anywhere = pl.BlockSpec(memory_space=pl.ANY)
        return pl.pallas_call(
            kernel,
            out_shape=(
                jax.ShapeDtypeStruct((rows, width), BF),
                jax.ShapeDtypeStruct((rows, width), BF),
                jax.ShapeDtypeStruct((4 * width, width), BF),
                jax.ShapeDtypeStruct((2 * width, width), BF),
                jax.ShapeDtypeStruct((16, width), F32),
            ),
            in_specs=[pl.BlockSpec(memory_space=pltpu.SMEM)] + [spec] * 7 + [anywhere] * 2,
            out_specs=(anywhere,) * 5,
            scratch_shapes=scratch,
            compiler_params=pltpu.CompilerParams(
                collective_id=0, has_side_effects=True, vmem_limit_bytes=62 * 1024 * 1024
            ),
        )(*operands)

    return call


def solution(mesh):
    dp_size, mp_size = mesh.shape["dp"], mesh.shape["mp"]

    def on_device(
        tokens, doc_starts, query_proj, key_proj, value_proj, query_bias, key_bias, value_bias,
        output_proj, output_bias, attn_gain, attn_shift, up_proj, up_bias, down_proj, down_bias,
        ffn_gain, ffn_shift, cotangent,
    ):
        _, rows, width = tokens.shape
        shard = up_proj.shape[1]
        blank = jnp.zeros((width,), F32)
        vec = jnp.stack(
            [query_bias, key_bias, value_bias, output_bias, attn_gain, attn_shift, down_bias,
             ffn_gain, ffn_shift] + [blank] * 6 + [up_bias]
        )
        call = build(dp_size, mp_size, rows, width, shard)
        layer_out, input_grad, attn, ff, small = call(
            doc_starts, tokens[0], cotangent[0], query_proj, key_proj, value_proj, output_proj,
            vec, up_proj, down_proj,
        )
        attn = attn.astype(F32).reshape(4, width, width)
        ff = ff.astype(F32).reshape(2, width, width)
        return (
            layer_out[None], input_grad[None], attn[0], attn[1], attn[2],
            small[0], small[1], small[2], attn[3], small[3], small[4], small[5],
            ff[0], small[15], ff[1], small[6], small[7], small[8],
        )

    rows_spec = P("dp", "mp", None)
    placed = (
        rows_spec, P("dp", None), P(), P(), P(), P(), P(), P(), P(), P(), P(), P(),
        P(None, "mp"), P("mp"), P("mp", None), P(), P(), P(), rows_spec,
    )
    results = (
        rows_spec, rows_spec, P(), P(), P(), P(), P(), P(), P(), P(), P(), P(),
        P(None, "mp"), P("mp"), P("mp", None), P(), P(), P(),
    )
    return jax.shard_map(
        on_device, mesh=mesh, in_specs=placed, out_specs=results, check_vma=False
    )
```

```python
import math

import jax
import jax.numpy as jnp
from jax import lax
from jax.experimental import pallas as pl
from jax.experimental.pallas import tpu as pltpu
from jax.sharding import PartitionSpec as P

HEADS = 12
HD = 64
SEQ = 1024
DOCS = 2
PAIR = 2 * HD
PAIRS = HEADS // 2
TILE = 256
MESH = pl.DeviceIdType.MESH
BF = jnp.bfloat16
F32 = jnp.float32
C0 = math.sqrt(2.0 / math.pi)
C1 = 0.044715


def mm(a, b):
    return lax.dot_general(a, b, (((1,), (0,)), ((), ())), preferred_element_type=F32)


def mm_nt(a, b):
    return lax.dot_general(a, b, (((1,), (1,)), ((), ())), preferred_element_type=F32)


def mm_tn(a, b):
    return lax.dot_general(a, b, (((0,), (0,)), ((), ())), preferred_element_type=F32)


def gelu_both(u):
    square = u * u
    t = jnp.tanh(C0 * u * (1.0 + C1 * square))
    half = 0.5 * (1.0 + t)
    slope = half + (0.5 * C0) * u * (1.0 - t * t) * (1.0 + (3.0 * C1) * square)
    return u * half, slope


def two_parts(x):
    high = x.astype(BF)
    return jnp.concatenate([high, (x - high.astype(F32)).astype(BF)], axis=1)


def col_sum(x):
    return jnp.sum(x, axis=0, keepdims=True)


def build(dp_size, mp_size, rows, width, shard):
    nbits = dp_size.bit_length() - 1
    nhalf = min(3, nbits)
    piece = width >> nhalf

    def order(kind):
        first = list(range(nhalf))
        if kind == 1 and nhalf == 3:
            first = [0, 2, 1]
        return first

    def w_order(kind):
        plain = order(kind)
        return plain[1:] + plain[:1]

    jobs = [order(k % 2) for k in range(8)]

    def kernel(
        starts, b_q, b_k, b_v, b_o, g_a, s_a, b_d, g_f, s_f, b_u,
        tok_hbm, cot_hbm, wq_hbm, wk_hbm, wv_hbm, wo_hbm, up_hbm, down_hbm,
        out_layer, out_input, out_q, out_k, out_v, out_o, out_up, out_down, out_small,
        tok, cot, wq, wk, wv, wo, vec, wu, wd, ub, rq, rk, vv, m2, mt2, cols, o2, bb, c1, ec, masks,
        state, state_in, ssum, ssum_in, grad_in, gsum_in, state_out, ssum_out, gsum_out,
        num, den, ctx, hid, rstd, normed, nf, mf, acted, gps, act2, upl2, zf, acc, mg, hlow, ngr,
        gq, gk, gv, part, gsum, red0, red1, red2, redx, zr, small, smallr, smallz, tokt, in_out,
        local_sem, send_sem, recv_sem,
    ):
        dp = lax.axis_index("dp")
        mp = lax.axis_index("mp")
        counter = [0]
        locals_used = [0]

        def bit(b):
            return lax.rem(lax.div(dp, 1 << b), 2)

        def flip(b):
            return {"dp": dp + (1 - 2 * bit(b)) * (1 << b)}

        def peer(r):
            return {"mp": lax.rem(mp + r, mp_size)}

        def across(i):
            other, span = mp, 1
            while span < mp_size:
                if i & span:
                    other = other + span * (1 - 2 * lax.rem(lax.div(mp, span), 2))
                span *= 2
            return other

        def remote(src, dst, device):
            i = counter[0]
            counter[0] += 1
            return pltpu.make_async_remote_copy(
                src_ref=src, dst_ref=dst, send_sem=send_sem.at[i], recv_sem=recv_sem.at[i],
                device_id=device, device_id_type=MESH,
            )

        def local(src, dst):
            i = locals_used[0]
            locals_used[0] += 1
            return pltpu.make_async_copy(src, dst, local_sem.at[i])

        def rds(start, size, unit=16):
            return pl.ds(pl.multiple_of(start, unit), size)

        barrier = pltpu.get_barrier_semaphore()
        for b in range(nbits):
            pl.semaphore_signal(barrier, inc=1, device_id=flip(b), device_id_type=MESH)
        for r in range(1, mp_size):
            pl.semaphore_signal(barrier, inc=1, device_id=peer(r), device_id_type=MESH)
        loads = {}
        for name, src, dst in (
            ("tok", tok_hbm, tok), ("q", wq_hbm, wq), ("k", wk_hbm, wk), ("v", wv_hbm, wv),
            ("o", wo_hbm, wo), ("up", up_hbm, wu.at[mp]), ("down", down_hbm, wd.at[mp]), ("cot", cot_hbm, cot),
        ):
            loads[name] = local(src, dst)
            loads[name].start()
        for index, source in enumerate((b_q, b_k, b_v, b_o, g_a, s_a, b_d, g_f, s_f)):
            vec[index : index + 1, :] = source[...].reshape(1, width)
        vec[15:16, :] = b_u[...].reshape(1, shard)
        ub[mp] = jnp.broadcast_to(vec[15:16, :], (8, shard))
        def w_base(kind, upto):
            bits = w_order(kind)
            base = 0
            for s in range(nhalf - 1, upto - 1, -1):
                base = base + bit(bits[s]) * (piece << s)
            return base

        half_cols = shard // 2

        def weight_job(kind, i, side):
            source, buf = ((up_hbm, wu), (down_hbm, wd))[kind]
            cols_at = pl.ds(side * half_cols, half_cols)
            at = rds(w_base(side, 0), piece)
            copy = remote(source.at[at, cols_at], buf.at[mp, at, cols_at], {"mp": across(i)})
            copy.start()
            yield
            for s in range(nhalf):
                copy.wait()
                ref = buf.at[across(i), rds(w_base(side, s), piece << s), cols_at]
                copy = remote(ref, ref, flip(w_order(side)[s]))
                copy.start()
                yield
            copy.wait()
            yield

        weight_jobs = {
            (kind, i, side): weight_job(kind, i, side)
            for kind in (0, 1) for i in range(1, mp_size) for side in (0, 1)
        }

        def pump(kind, which=range(1, mp_size)):
            for i in which:
                for side in (0, 1):
                    next(weight_jobs[kind, i, side])

        own_start = mp * rows

        def layout(places):
            opened = jnp.full(places.shape, 0, jnp.int32) + starts[0, 0]
            closed = jnp.full(places.shape, SEQ, jnp.int32)
            if DOCS > 1:
                closed = jnp.full(places.shape, 0, jnp.int32) + starts[0, 1]
            number = jnp.zeros(places.shape, jnp.int32)
            for d in range(1, DOCS):
                ending = starts[0, d + 1] if d + 1 < DOCS else SEQ
                inside = places >= starts[0, d]
                opened = jnp.where(inside, starts[0, d], opened)
                closed = jnp.where(inside, ending, closed)
                number = number + inside.astype(jnp.int32)
            angles = (places - opened).astype(F32) * (0.5 * math.pi) / (closed - opened).astype(F32)
            return number, jnp.cos(angles), jnp.sin(angles)

        places = own_start + lax.broadcasted_iota(jnp.int32, (rows, 128), 0)
        number_c, cos_c, sin_c = layout(places)
        row_places = own_start + lax.broadcasted_iota(jnp.int32, (8, rows), 1)
        number_r, cos_r, sin_r = layout(row_places)
        edge = jnp.zeros((8, 128), jnp.int32)
        last, _, _ = layout(edge + own_start + (rows - 1))
        before, _, _ = layout(edge + own_start - 1)
        has_prev = jnp.where(edge + mp > 0, 1.0, 0.0)
        carried = jnp.where(number_c == before[:1], 1.0, 0.0) * has_prev[:1]
        in_last = jnp.where(number_c == last[:1], 1.0, 0.0)
        linked = (jnp.where(before == last, 1.0, 0.0) * has_prev)[:1]
        cols[0] = cos_c * carried
        cols[1] = sin_c * carried
        cols[2] = cos_c * in_last
        cols[3] = sin_c * in_last
        linked2 = jnp.concatenate([linked, linked], axis=1)
        linked6 = jnp.concatenate([linked] * (width // 128), axis=1)
        wide = jnp.concatenate([number_c, number_c], axis=1)
        wide_cos = jnp.concatenate([cos_c, cos_c], axis=1)
        wide_sin = jnp.concatenate([sin_c, sin_c], axis=1)
        row_id = lax.broadcasted_iota(jnp.int32, (rows, rows), 0)
        col_id = lax.broadcasted_iota(jnp.int32, (rows, rows), 1)
        angle_gap = wide_cos * cos_r[:1] + wide_sin * sin_r[:1]
        same = wide == number_r[:1]
        lower = jnp.where(same & (col_id <= row_id), angle_gap, 0.0)
        upper_part = jnp.where(same & (col_id >= row_id), angle_gap, 0.0)
        m2[:, :rows] = lower
        m2[:, rows:] = lower
        mt2[:, :rows] = upper_part
        mt2[:, rows:] = upper_part

        lane = lax.broadcasted_iota(jnp.int32, (rows, PAIR), 1)
        low_f = jnp.where(lane < HD, 1.0, 0.0)
        high_f = 1.0 - low_f
        first_two = jnp.where(lax.rem(lane, HD) < 2, 1.0, 0.0)
        o2[:rows, :] = low_f.astype(BF)
        o2[rows:, :] = high_f.astype(BF)
        c1[:rows, :] = (first_two * low_f).astype(BF)
        c1[rows:, :] = (first_two * high_f).astype(BF)
        ec[...] = first_two.astype(BF)
        block_row = lax.broadcasted_iota(jnp.int32, (2 * PAIR, PAIR), 0)
        block_col = lax.broadcasted_iota(jnp.int32, (2 * PAIR, PAIR), 1)
        bb[...] = jnp.where(
            lax.div(lax.rem(block_row, PAIR), HD) == lax.div(block_col, HD), 1.0, 0.0
        ).astype(BF)
        lo = low_f.astype(BF)[:16]
        hi = high_f.astype(BF)[:16]
        masks[0] = lo
        masks[1] = hi
        masks[2] = jnp.where(lax.rem(lane, HD) == 0, 1.0, 0.0).astype(BF)[:16]
        masks[3] = jnp.where(lax.rem(lane, HD) == 1, 1.0, 0.0).astype(BF)[:16]

        def halves(x):
            return jnp.concatenate([x * masks[0, :1], x * masks[1, :1]], axis=0)

        def expand(compact):
            low4 = jnp.concatenate([masks[0, :1]] * 2, axis=1)
            high4 = jnp.concatenate([masks[1, :1]] * 2, axis=1)
            return jnp.concatenate([compact * low4, compact * high4], axis=0)

        def compact_of(full):
            low4 = jnp.concatenate([masks[0, :1]] * 2, axis=1).astype(F32)
            high4 = jnp.concatenate([masks[1, :1]] * 2, axis=1).astype(F32)
            return full[:HD] * low4 + full[HD:] * high4

        def project(weight, out, name, row):
            loads[name].wait()
            for j in range(width // TILE):
                at = pl.ds(j * TILE, TILE)
                y = mm(tok[...], weight[:, at]) + vec[row : row + 1, at]
                if row < 2:
                    y = jnp.maximum(y, 0.0)
                out[:, at] = y.astype(BF)

        loads["tok"].wait()
        project(wk, rk, "k", 1)
        project(wv, vv, "v", 2)

        def lanes(p):
            return pl.ds(pl.multiple_of(p * PAIR, PAIR), PAIR)

        def feats(ref, p, which):
            x = ref[:, lanes(p)].astype(F32)
            return (x * cols[which]).astype(BF), (x * cols[which + 1]).astype(BF)

        def contribs(p, carry):
            kc, ks = feats(rk, p, 2)
            full = mm_tn(vv[:, lanes(p)], jnp.concatenate([kc, ks], axis=1))
            state[p] = compact_of(full)
            ssum[0:1, lanes(p)] = col_sum(kc.astype(F32))
            ssum[1:2, lanes(p)] = col_sum(ks.astype(F32))
            return carry

        ssum[...] = jnp.zeros_like(ssum)
        lax.fori_loop(0, PAIRS, contribs, 0)

        CH = 3
        PC = PAIRS // CH

        class Chain:
            def __init__(self, out_state, out_sum, in_state, in_sum, forward):
                step = 1 if forward else mp_size - 1
                self.has_in = (mp > 0) if forward else (mp < mp_size - 1)
                self.has_out = (mp < mp_size - 1) if forward else (mp > 0)
                self.rank = mp if forward else mp_size - 1 - mp
                self.refs = out_state, out_sum, in_state, in_sum
                self.copies = [
                    remote(out_state.at[pl.ds(c * PC, PC)], in_state.at[pl.ds(c * PC, PC)], peer(step))
                    for c in range(CH)
                ]
                self.sum_copy = remote(out_sum, in_sum, peer(step))

            def early(self):
                out_state, out_sum, in_state, in_sum = self.refs

                @pl.when(jnp.logical_not(self.has_in))
                def _():
                    in_state[...] = jnp.zeros_like(in_state)
                    in_sum[...] = jnp.zeros_like(in_sum)
                    out_sum[...] = ssum[...]
                    self.sum_copy.start()
                    for c in range(CH):
                        at = pl.ds(c * PC, PC)
                        out_state[at] = state[at].astype(BF)
                        self.copies[c].start()

            def slot(self, k):
                for c in range(CH):
                    if 0 <= k - c <= mp_size - 2:
                        self.service(c, self.rank == k - c + 1)

            def service(self, c, here):
                out_state, out_sum, in_state, in_sum = self.refs

                @pl.when(here)
                def _():
                    if c == 0:
                        self.sum_copy.wait_recv()

                        @pl.when(self.has_out)
                        def _():
                            out_sum[...] = ssum[...] + in_sum[...] * linked6
                            self.sum_copy.start()

                    self.copies[c].wait_recv()

                    @pl.when(self.has_out)
                    def _():
                        for p in range(c * PC, (c + 1) * PC):
                            out_state[p] = (state[p] + in_state[p].astype(F32) * linked2).astype(BF)
                        self.copies[c].start()

            def finish(self):
                @pl.when(self.has_out)
                def _():
                    for copy in self.copies + [self.sum_copy]:
                        copy.wait_send()

        ahead = Chain(state_out, ssum_out, state_in, ssum_in, True)
        behind = Chain(state_out, gsum_out, grad_in, gsum_in, False)
        neighbour = {"mp": across(1)}
        norm_pair = remote(nf.at[pl.ds(0, rows)], nf.at[pl.ds(rows, rows)], neighbour)
        merged_pair = remote(mf.at[pl.ds(0, rows)], mf.at[pl.ds(rows, rows)], neighbour)
        pl.semaphore_wait(barrier, nbits + mp_size - 1)
        pump(0)
        ahead.early()
        bias_copies = [remote(ub.at[mp], ub.at[mp], {"mp": across(i)}) for i in range(1, mp_size)]
        for copy in bias_copies:
            copy.start()
        project(wq, rq, "q", 0)
        flow = [(k, i) for k in (0, 1) for i in range(1, mp_size)]

        def wave(d):
            for stage in range(nhalf + 1):
                if 0 <= d - stage < len(flow):
                    kind, i = flow[d - stage]
                    pump(kind, [i])

        def local_attention(p, carry):
            k2 = halves(rk[:, lanes(p)])
            a = (mm_nt(rq[:, lanes(p)], k2) * m2[...]).astype(BF)
            both = mm(a, jnp.concatenate([halves(vv[:, lanes(p)]), o2[...]], axis=1))
            num[:, lanes(p)] = both[:, :PAIR]
            den[:, lanes(p)] = both[:, PAIR:]
            return carry

        for c in range(CH):
            lax.fori_loop(c * PC, (c + 1) * PC, local_attention, 0)
            wave(c)
            pump(1, [c + 1])
            ahead.slot(c)
        wave(3)
        ahead.slot(3)
        wave(4)
        ahead.slot(4)

        def remote_attention(p, carry):
            at = lanes(p)
            qc, qs = feats(rq, p, 0)
            carry_num = mm_nt(jnp.concatenate([qc, qs], axis=1), expand(state_in[p]))
            weighted = qc.astype(F32) * ssum_in[0:1, at] + qs.astype(F32) * ssum_in[1:2, at]
            total = den[:, at] + mm(two_parts(weighted), bb[...])
            value = (num[:, at] + carry_num) / jnp.maximum(total, 1.0)
            den[:, at] = total
            num[:, at] = value
            ctx[:, at] = value.astype(BF)
            return carry

        lax.fori_loop(0, PAIRS, remote_attention, 0)

        loads["o"].wait()
        for j in range(width // TILE):
            at = pl.ds(j * TILE, TILE)
            hid[:, at] = tok[:, at].astype(F32) + mm(ctx[...], wo[:, at]) + vec[3:4, at]
        RB = 64

        def first_norm(i, carry):
            at = pl.ds(pl.multiple_of(i * RB, RB), RB)
            x = hid[at, :]
            center = x - jnp.mean(x, axis=1, keepdims=True)
            inv = lax.rsqrt(jnp.mean(center * center, axis=1, keepdims=True) + 1e-05)
            xhat = center * inv
            y = xhat * vec[4:5, :] + vec[5:6, :]
            hid[at, :] = xhat
            rstd[at, :] = jnp.broadcast_to(inv, (RB, 128))
            normed[at, :] = y
            nf[at, :] = y.astype(BF)
            return carry

        lax.fori_loop(0, rows // RB, first_norm, 0)
        norm_pair.start()

        def ffn_up(t):
            for j in range(shard // TILE):
                at = pl.ds(j * TILE, TILE)
                u = mm(nf[:rows, :], wu[t, :, at]) + ub[t, 0:1, at]
                value, slope = gelu_both(u)
                acted[t, :, at] = value.astype(BF)
                gps[t, :, at] = slope

        def ffn_down(t, first):
            for j in range(width // TILE):
                at = pl.ds(j * TILE, TILE)
                y = mm(acted[t], wd[t, :, at])
                if first:
                    acc[:, at] = y
                else:
                    acc[:, at] += y

        loads["up"].wait()
        loads["down"].wait()
        for copy in bias_copies:
            copy.wait()
        ffn_up(mp)
        wave(5)
        ffn_up(across(1))
        ffn_up(across(2))
        ffn_up(across(3))
        ffn_down(mp, True)
        wave(6)
        ffn_down(across(1), False)
        wave(7)
        ffn_down(across(2), False)
        wave(8)
        ffn_down(across(3), False)
        small[0] = jnp.zeros_like(small[0])
        loads["cot"].wait()

        def second_norm(i, carry):
            at = pl.ds(pl.multiple_of(i * RB, RB), RB)
            x = normed[at, :] + acc[at, :] + vec[6:7, :]
            center = x - jnp.mean(x, axis=1, keepdims=True)
            inv = lax.rsqrt(jnp.mean(center * center, axis=1, keepdims=True) + 1e-05)
            xhat = center * inv
            in_out[0, at, :] = (xhat * vec[7:8, :] + vec[8:9, :]).astype(BF)
            g = cot[at, :].astype(F32)
            s = g * vec[7:8, :]
            grad = (
                s - jnp.mean(s, axis=1, keepdims=True) - xhat * jnp.mean(s * xhat, axis=1, keepdims=True)
            ) * inv
            mg[at, :] = grad
            mf[at, :] = grad.astype(BF)
            small[0, 7:8, :] += col_sum(g * xhat)
            small[0, 8:9, :] += col_sum(g)
            small[0, 6:7, :] += col_sum(grad)
            return carry

        lax.fori_loop(0, rows // RB, second_norm, 0)
        layer_copy = local(in_out.at[0], out_layer)
        layer_copy.start()
        merged_pair.start()

        def ffn_back(r, carry):
            t = lax.rem(mp + r, mp_size)
            for j in range(shard // TILE):
                at = pl.ds(j * TILE, TILE)
                up_grad = mm_nt(mf[:rows, :], wd[t, at, :]) * gps[t, :, at]
                upl2[:rows, at] = up_grad.astype(BF)
            for j in range(width // TILE):
                at = pl.ds(j * TILE, TILE)
                mg[:, at] += mm_nt(upl2[:rows, :], wu[t, at, :])
            return carry

        lax.fori_loop(0, mp_size, ffn_back, 0)

        def norm_back(i, carry):
            at = pl.ds(pl.multiple_of(i * RB, RB), RB)
            g = mg[at, :]
            xhat = hid[at, :]
            s = g * vec[4:5, :]
            inv = rstd[at, 0:1]
            grad = (
                s - jnp.mean(s, axis=1, keepdims=True) - xhat * jnp.mean(s * xhat, axis=1, keepdims=True)
            ) * inv
            acc[at, :] = grad
            hlow[at, :] = grad.astype(BF)
            small[0, 4:5, :] += col_sum(g * xhat)
            small[0, 5:6, :] += col_sum(g)
            small[0, 3:4, :] += col_sum(grad)
            return carry

        lax.fori_loop(0, rows // RB, norm_back, 0)
        for j in range(width // TILE):
            at = pl.ds(j * TILE, TILE)
            gv[:, at] = mm_nt(hlow[...], wo[at, :]).astype(BF)

        def back_state(p, carry):
            at = lanes(p)
            total = den[:, at]
            inv = 1.0 / jnp.maximum(total, 1.0)
            g = gv[:, at].astype(F32)
            numer = (g * inv).astype(BF)
            sums = mm(two_parts(g * num[:, at]), bb[...])
            den_grad = jnp.where(total > 1.0, -sums * inv, 0.0)
            ngr[:, at] = numer
            mg[:, at] = den_grad
            qc, qs = feats(rq, p, 0)
            full = mm_tn(numer, jnp.concatenate([qc, qs], axis=1))
            state[p] = compact_of(full)
            ssum[0:1, at] = col_sum(qc.astype(F32) * den_grad)
            ssum[1:2, at] = col_sum(qs.astype(F32) * den_grad)
            return carry

        ssum[...] = jnp.zeros_like(ssum)
        ahead.finish()
        lax.fori_loop(0, PAIRS, back_state, 0)
        behind.early()

        def weight_grad(index, left_t, right):
            def body(i, carry):
                at = rds(i * TILE, TILE, TILE)
                for j in range(width // TILE):
                    to = pl.ds(j * TILE, TILE)
                    part[rds(index * width + i * TILE, TILE, TILE), to] = mm(
                        left_t[at, :], right[:, to]
                    ).astype(BF)
                return carry

            lax.fori_loop(0, width // TILE, body, 0)


        def j_base(job, upto):
            base = 0
            for s in range(upto):
                base = base + bit(jobs[job][s]) * (width >> (s + 1))
            return base

        reds = [red0, red1, red2]

        def part_of(job):
            if job < 4:
                return part.at[pl.ds(job * width, width)]
            return (wu, wd)[job % 2].at[across((1, 3)[(job - 4) // 2])]

        def add_rows(ref, start, count, received):
            step = min(count, 96)

            def body(i, carry):
                at = rds(start + i * step, step)
                ref[at, :] = (
                    ref[at, :].astype(F32) + received[rds(i * step, step), :].astype(F32)
                ).astype(BF)
                return carry

            lax.fori_loop(0, count // step, body, 0)

        def scatter_job(job):
            ref = part_of(job)
            for s in range(nhalf):
                half = width >> (s + 1)
                b = jobs[job][s]
                away = j_base(job, s) + (1 - bit(b)) * half
                copy = remote(ref.at[rds(away, half)], reds[s].at[job], flip(b))
                copy.start()
                yield
                copy.wait()
                add_rows(ref, j_base(job, s + 1), half, reds[s].at[job])
            for e, b in enumerate(range(nhalf, nbits)):
                at = rds(j_base(job, nhalf), piece)
                copy = remote(ref.at[at], redx.at[job, e], flip(b))
                copy.start()
                copy.wait()
                add_rows(ref, j_base(job, nhalf), piece, redx.at[job, e])
            yield

        outs = [out_q, out_o, out_v, out_k, out_up, out_down]
        final_copies = []

        def gather_job(job):
            for s in range(nhalf - 1, -1, -1):
                at = rds(job * width + j_base(job, s + 1), width >> (s + 1))
                copy = remote(gsum.at[at], gsum.at[at], flip(jobs[job][s]))
                copy.start()
                yield
                copy.wait()
            out = local(gsum.at[pl.ds(job * width, width)], outs[job])
            out.start()
            final_copies.append(out)
            yield

        quarter = piece // 2

        def quarter_row(first, t):
            which = lax.div(t, 2)
            base = (1 - which) * j_base(first, nhalf) + which * j_base(first + 1, nhalf)
            return (first + which) * width + base + lax.rem(t, 2) * quarter

        def z_job(first, slot):
            copies = []
            for i in range(1, mp_size):
                copies.append(
                    remote(
                        part.at[rds(quarter_row(first, across(i)), quarter)],
                        zr.at[slot, i - 1], {"mp": across(i)},
                    )
                )
                copies[-1].start()
            yield
            for copy in copies:
                copy.wait()
            at = rds(quarter_row(first, mp), quarter)
            total = part[at, :].astype(F32)
            for i in range(mp_size - 1):
                total = total + zr[slot, i].astype(F32)
            gsum[at, :] = total.astype(BF)
            copies = [remote(gsum.at[at], gsum.at[at], {"mp": across(i)}) for i in range(1, mp_size)]
            for copy in copies:
                copy.start()
            yield
            for copy in copies:
                copy.wait()
            yield

        def small_job():
            for b in range(nbits):
                copy = remote(small.at[b], smallr.at[b], flip(b))
                copy.start()
                yield
                copy.wait()
                small[b + 1] = small[b] + smallr[b]
            smallz[mp] = small[nbits]
            copies = [remote(smallz.at[mp], smallz.at[mp], {"mp": across(i)}) for i in range(1, mp_size)]
            for copy in copies:
                copy.start()
            yield
            for copy in copies:
                copy.wait()
            total = smallz[0]
            for z in range(1, mp_size):
                total = total + smallz[z]
            smallr[0, 0:8] = total[0:8]
            smallr[0, 8:16] = total[8:16]
            smallr[0, 15:16] = smallz[mp, 15:16] + smallz[across(2), 14:15]
            out = local(smallr.at[0], out_small)
            out.start()
            final_copies.append(out)
            yield

        def ff_z_job():
            copies = []
            for slot, job in enumerate((UB, DB)):
                at = rds(j_base(job, nhalf), piece)
                copies.append(remote(part_of(job).at[at], zf.at[slot], {"mp": across(2)}))
                copies[-1].start()
            yield
            for copy in copies:
                copy.wait()
            for slot, job in enumerate((UA, DA)):
                total = part_of(job)[rds(j_base(job, nhalf), piece), :].astype(F32) + zf[slot].astype(F32)
                gsum[rds(job * width + j_base(job, nhalf), piece), :] = total.astype(BF)
            yield

        Q, O, V, K, UA, DA, UB, DB = range(8)
        ff_z = ff_z_job()
        scatter = [scatter_job(job) for job in range(8)]
        gather = [gather_job(job) for job in range(6)]
        z_first = z_job(Q, 0)
        z_second = z_job(V, 1)
        smalls = small_job()

        def step(*generators):
            for g in generators:
                assert next(g, 1) is None

        tokt[...] = ctx[...].T
        weight_grad(O, tokt, hlow)
        step(scatter[O])

        def back_local(p, carry):
            at = lanes(p)
            qp = rq[:, at]
            kp = rk[:, at]
            vp = vv[:, at]
            numer = ngr[:, at]
            den_grad = mg[:, at]
            k2 = halves(kp)
            q2 = halves(qp)
            n2 = halves(numer)
            dh = den_grad.astype(BF)
            dl = (den_grad - dh.astype(F32)).astype(BF)
            x = dh * masks[2, :1] + dl * masks[3, :1]
            ds = (
                mm_nt(
                    jnp.concatenate([numer, x], axis=1),
                    jnp.concatenate([halves(vp), c1[...]], axis=1),
                )
                * m2[...]
            ).astype(BF)
            grad_q = mm(ds, k2)
            at_scores = (mm_nt(kp, q2) * mt2[...]).astype(BF)
            gv_part = mm(at_scores, n2)
            dst = (
                mm_nt(
                    jnp.concatenate([vp, ec[...]], axis=1),
                    jnp.concatenate([n2, halves(x)], axis=1),
                )
                * mt2[...]
            ).astype(BF)
            gk_part = mm(dst, q2)
            t = mm(numer, expand(state_in[p]))
            cq = cols[0]
            sq = cols[1]
            grad_q = grad_q + cq * t[:, :PAIR] + sq * t[:, PAIR:]
            grad_q = grad_q + den_grad * (cq * ssum_in[0:1, at] + sq * ssum_in[1:2, at])
            grad_q = jnp.where(qp.astype(F32) > 0.0, grad_q, 0.0)
            small[0, 0:1, at] = col_sum(grad_q)
            gq[:, at] = grad_q.astype(BF)
            normed[:, at] = gk_part
            hid[:, at] = gv_part
            return carry

        for c in range(CH):
            lax.fori_loop(c * PC, (c + 1) * PC, back_local, 0)
            behind.service(c, behind.has_in)
        step(scatter[O])
        tokt[...] = tok[...].T
        weight_grad(Q, tokt, gq)
        step(scatter[Q])

        def back_remote(p, carry):
            at = lanes(p)
            full = expand(grad_in[p])
            t = mm(vv[:, at], full)
            kc, ks = feats(rk, p, 2)
            ck = cols[2]
            sk = cols[3]
            grad_k = normed[:, at] + ck * (t[:, :PAIR] + gsum_in[0:1, at]) + sk * (
                t[:, PAIR:] + gsum_in[1:2, at]
            )
            grad_k = jnp.where(rk[:, at].astype(F32) > 0.0, grad_k, 0.0)
            small[0, 1:2, at] = col_sum(grad_k)
            gk[:, at] = grad_k.astype(BF)
            grad_v = hid[:, at] + mm_nt(jnp.concatenate([kc, ks], axis=1), full)
            small[0, 2:3, at] = col_sum(grad_v)
            gv[:, at] = grad_v.astype(BF)
            return carry

        lax.fori_loop(0, PAIRS, back_remote, 0)
        weight_grad(K, tokt, gk)
        step(scatter[K])
        weight_grad(V, tokt, gv)
        step(scatter[V], scatter[Q], scatter[O], scatter[K])

        for j in range(width // TILE):
            at = pl.ds(j * TILE, TILE)
            total = acc[:, at] + mm_nt(gq[...], wq[at, :]) + mm_nt(gk[...], wk[at, :])
            in_out[1, :, at] = (total + mm_nt(gv[...], wv[at, :])).astype(BF)
        input_copy = local(in_out.at[1], out_input)
        input_copy.start()
        step(scatter[V], scatter[Q], scatter[O])

        norm_pair.wait()
        merged_pair.wait()

        def shard_grads(t, up_job, down_job, row):
            for j in range(shard // TILE):
                at = pl.ds(j * TILE, TILE)
                u = mm(nf[...], wu[t, :, at]) + ub[t, 0:1, at]
                value, slope = gelu_both(u)
                up_grad = mm_nt(mf[...], wd[t, at, :]) * slope
                small[0, row : row + 1, at] = col_sum(up_grad)
                act2[:, at] = value.astype(BF)
                upl2[:, at] = up_grad.astype(BF)
            for j in range(width // TILE):
                at = pl.ds(j * TILE, TILE)
                part_of(up_job)[pl.ds(j * TILE, TILE), :] = mm_tn(nf[:, at], upl2[...]).astype(BF)
            for j in range(shard // TILE):
                at = pl.ds(j * TILE, TILE)
                part_of(down_job)[pl.ds(j * TILE, TILE), :] = mm_tn(act2[:, at], mf[...]).astype(BF)

        shard_grads(across(2), UB, DB, 14)
        step(scatter[UB], scatter[DB])
        step(scatter[Q])
        step(z_first, scatter[V], scatter[K])
        shard_grads(mp, UA, DA, 15)
        step(scatter[UA], scatter[DA], smalls)
        step(z_first)
        step(scatter[UB], scatter[DB])
        step(scatter[V], scatter[K], z_second)
        step(scatter[UA], scatter[DA], smalls)
        step(z_first, gather[Q], gather[O])
        step(scatter[UB], scatter[DB], z_second)
        step(scatter[UA], scatter[DA], smalls)
        step(gather[Q], gather[O])
        step(z_second, gather[V], gather[K])
        step(scatter[UB], scatter[DB], ff_z)
        step(gather[Q], gather[O], smalls)
        step(gather[V], gather[K])
        step(scatter[UA], scatter[DA], ff_z, gather[UA], gather[DA])
        step(gather[Q], gather[O])
        step(gather[V], gather[K], smalls)
        step(gather[UA], gather[DA])
        step(gather[V], gather[K])
        step(gather[UA], gather[DA])
        step(gather[UA], gather[DA])
        for _ in smalls:
            pass
        for g in scatter + gather + [z_first, z_second, ff_z, smalls] + list(weight_jobs.values()):
            assert next(g, 1) == 1
        behind.finish()
        layer_copy.wait()
        input_copy.wait()
        for copy in final_copies:
            copy.wait()

    def call(*operands):
        vm = pltpu.VMEM
        big = lambda *s: vm(s, BF)
        flt = lambda *s: vm(s, F32)
        nsem = 224
        square = jax.ShapeDtypeStruct((width, width), BF)
        scratch = [
            big(rows, width), big(rows, width), big(width, width), big(width, width), big(width, width),
            big(width, width), flt(16, width),
            big(mp_size, width, shard), big(mp_size, shard, width), flt(mp_size, 8, shard),
            big(rows, width), big(rows, width), big(rows, width),
            flt(rows, 2 * rows), flt(rows, 2 * rows), flt(4, rows, 128),
            big(2 * rows, PAIR), big(2 * PAIR, PAIR), big(2 * rows, PAIR), big(rows, PAIR), big(4, 16, PAIR),
            flt(PAIRS, HD, 2 * PAIR), big(PAIRS, HD, 2 * PAIR), flt(8, width), flt(8, width),
            big(PAIRS, HD, 2 * PAIR), flt(8, width), big(PAIRS, HD, 2 * PAIR), flt(8, width),
            flt(8, width),
            flt(rows, width), flt(rows, width), big(rows, width), flt(rows, width), flt(rows, 128),
            flt(rows, width), big(2 * rows, width), big(2 * rows, width),
            big(mp_size, rows, shard), flt(mp_size, rows, shard), big(2 * rows, shard), big(2 * rows, shard),
            big(2, piece, width), flt(rows, width), flt(rows, width),
            big(rows, width), big(rows, width),
            big(rows, width), big(rows, width), big(rows, width),
            big(4 * width, width), big(6 * width, width),
            big(8, width // 2, width), big(8, width // 4, width), big(8, width // 8, width),
            big(8, max(1, nbits - nhalf), 16 if nbits == nhalf else piece, width), big(2, mp_size - 1, piece // 2, width),
            flt(nbits + 1, 16, width), flt(nbits, 16, width), flt(mp_size, 16, width),
            big(width, rows), big(2, rows, width),
            pltpu.SemaphoreType.DMA((32,)), pltpu.SemaphoreType.DMA((nsem,)), pltpu.SemaphoreType.DMA((nsem,)),
        ]
        spec = pl.BlockSpec(memory_space=pltpu.VMEM)
        anywhere = pl.BlockSpec(memory_space=pl.ANY)
        return pl.pallas_call(
            kernel,
            out_shape=(
                jax.ShapeDtypeStruct((rows, width), BF),
                jax.ShapeDtypeStruct((rows, width), BF),
                square, square, square, square, square, square,
                jax.ShapeDtypeStruct((16, width), F32),
            ),
            in_specs=[pl.BlockSpec(memory_space=pltpu.SMEM)] + [spec] * 10 + [anywhere] * 8,
            out_specs=(anywhere,) * 9,
            scratch_shapes=scratch,
            compiler_params=pltpu.CompilerParams(
                collective_id=0, has_side_effects=True, vmem_limit_bytes=63 * 1024 * 1024
            ),
        )(*operands)

    return call


def widen(layer, back, grads, small):
    rows, width = layer.shape
    steps = 8

    def kernel(*refs):
        n = len(grads)
        ins, outs = refs[: n + 3], refs[n + 3 :]
        outs[0][...] = ins[0][...]
        outs[1][...] = ins[1][...]
        for g in range(n):
            outs[2 + g][...] = ins[2 + g][...].astype(F32)

        @pl.when(pl.program_id(0) == 0)
        def _():
            for row, out in zip((0, 1, 2, 3, 4, 5, 15, 6, 7, 8), outs[2 + n :]):
                out[...] = ins[2 + n][row : row + 1, :].reshape(width)

    block = lambda x: pl.BlockSpec((x.shape[0] // steps, x.shape[1]), lambda i: (i, 0))
    whole = pl.BlockSpec(small.shape, lambda i: (0, 0))
    vector = pl.BlockSpec((width,), lambda i: (0,))
    mats = [layer, back, *grads]
    return pl.pallas_call(
        kernel,
        grid=(steps,),
        in_specs=[block(x) for x in mats] + [whole],
        out_specs=[block(x) for x in mats] + [vector] * 10,
        out_shape=[jax.ShapeDtypeStruct(x.shape, BF) for x in (layer, back)]
        + [jax.ShapeDtypeStruct(x.shape, F32) for x in grads]
        + [jax.ShapeDtypeStruct((width,), F32)] * 10,
        compiler_params=pltpu.CompilerParams(vmem_limit_bytes=62 * 1024 * 1024),
    )(*mats, small)


def solution(mesh):
    dp_size, mp_size = mesh.shape["dp"], mesh.shape["mp"]

    def on_device(
        tokens, doc_starts, query_proj, key_proj, value_proj, query_bias, key_bias, value_bias,
        output_proj, output_bias, attn_gain, attn_shift, up_proj, up_bias, down_proj, down_bias,
        ffn_gain, ffn_shift, cotangent,
    ):
        _, rows, width = tokens.shape
        shard = up_proj.shape[1]
        call = build(dp_size, mp_size, rows, width, shard)
        layer_out, input_grad, gq, gk, gv, go, gu, gd, small = call(
            doc_starts, query_bias, key_bias, value_bias, output_bias, attn_gain, attn_shift,
            down_bias, ffn_gain, ffn_shift, up_bias, tokens[0], cotangent[0],
            query_proj, key_proj, value_proj, output_proj, up_proj, down_proj,
        )
        layer_out, input_grad, gq, gk, gv, go, gu, gd, *vecs = widen(
            layer_out, input_grad, (gq, gk, gv, go, gu, gd), small
        )
        bq, bk, bv, bo, ga, sa, bu, bd, gf, sf = vecs
        return (
            layer_out[None], input_grad[None], gq, gk, gv, bq, bk, bv, go, bo, ga, sa,
            gu, bu, gd, bd, gf, sf,
        )

    rows_spec = P("dp", "mp", None)
    placed = (
        rows_spec, P("dp", None), P(), P(), P(), P(), P(), P(), P(), P(), P(), P(),
        P(None, "mp"), P("mp"), P("mp", None), P(), P(), P(), rows_spec,
    )
    results = (
        rows_spec, rows_spec, P(), P(), P(), P(), P(), P(), P(), P(), P(), P(),
        P(None, "mp"), P("mp"), P("mp", None), P(), P(), P(),
    )
    return jax.shard_map(
        on_device, mesh=mesh, in_specs=placed, out_specs=results, check_vma=False
    )
```

```python
import math

import jax
import jax.numpy as jnp
from jax import lax
from jax.experimental import pallas as pl
from jax.experimental.pallas import tpu as pltpu
from jax.sharding import PartitionSpec as P

HEADS = 12
HD = 64
SEQ = 1024
DOCS = 2
PAIR = 2 * HD
PAIRS = HEADS // 2
TILE = 256
MESH = pl.DeviceIdType.MESH
BF = jnp.bfloat16
F32 = jnp.float32
C0 = math.sqrt(2.0 / math.pi)
C1 = 0.044715


def mm(a, b):
    return lax.dot_general(a, b, (((1,), (0,)), ((), ())), preferred_element_type=F32)


def mm_nt(a, b):
    return lax.dot_general(a, b, (((1,), (1,)), ((), ())), preferred_element_type=F32)


def mm_tn(a, b):
    return lax.dot_general(a, b, (((0,), (0,)), ((), ())), preferred_element_type=F32)


def gelu_both(u):
    square = u * u
    t = jnp.tanh(C0 * u * (1.0 + C1 * square))
    half = 0.5 * (1.0 + t)
    slope = half + (0.5 * C0) * u * (1.0 - t * t) * (1.0 + (3.0 * C1) * square)
    return u * half, slope


def two_parts(x):
    high = x.astype(BF)
    return jnp.concatenate([high, (x - high.astype(F32)).astype(BF)], axis=1)


def col_sum(x):
    return jnp.sum(x, axis=0, keepdims=True)


def build(dp_size, mp_size, rows, width, shard):
    nbits = dp_size.bit_length() - 1
    nhalf = min(3, nbits)
    piece = width >> nhalf

    def order(kind):
        first = list(range(nhalf))
        if kind == 1 and nhalf == 3:
            first = [0, 2, 1]
        return first

    def w_order(kind):
        plain = order(kind)
        return plain[1:] + plain[:1]

    jobs = [order(k % 2) for k in range(8)]

    def kernel(
        starts, b_q, b_k, b_v, b_o, g_a, s_a, b_d, g_f, s_f, b_u,
        tok_hbm, cot_hbm, wq_hbm, wk_hbm, wv_hbm, wo_hbm, up_hbm, down_hbm,
        out_layer, out_input, out_q, out_k, out_v, out_o, out_up, out_down, out_small,
        tok, cot, wq, wk, wv, wo, vec, wu, wd, ub, rq, rk, vv, m2, mt2, cols, o2, bb, c1, ec, masks,
        state, state_in, ssum, ssum_in, grad_in, gsum_in, state_out, ssum_out, gsum_out,
        num, den, ctx, hid, rstd, normed, nf, mf, acted, gps, act2, upl2, zf, acc, mg, hlow, ngr,
        gq, gk, gv, part, gsum, red0, red1, red2, redx, zr, small, smallr, smallz, tokt, in_out,
        local_sem, send_sem, recv_sem,
    ):
        dp = lax.axis_index("dp")
        mp = lax.axis_index("mp")
        counter = [0]
        locals_used = [0]

        def bit(b):
            return lax.rem(lax.div(dp, 1 << b), 2)

        def flip(b):
            return {"dp": dp + (1 - 2 * bit(b)) * (1 << b)}

        def peer(r):
            return {"mp": lax.rem(mp + r, mp_size)}

        def across(i):
            other, span = mp, 1
            while span < mp_size:
                if i & span:
                    other = other + span * (1 - 2 * lax.rem(lax.div(mp, span), 2))
                span *= 2
            return other

        def remote(src, dst, device):
            i = counter[0]
            counter[0] += 1
            return pltpu.make_async_remote_copy(
                src_ref=src, dst_ref=dst, send_sem=send_sem.at[i], recv_sem=recv_sem.at[i],
                device_id=device, device_id_type=MESH,
            )

        def local(src, dst):
            i = locals_used[0]
            locals_used[0] += 1
            return pltpu.make_async_copy(src, dst, local_sem.at[i])

        def rds(start, size, unit=16):
            return pl.ds(pl.multiple_of(start, unit), size)

        barrier = pltpu.get_barrier_semaphore()
        for b in range(nbits):
            pl.semaphore_signal(barrier, inc=1, device_id=flip(b), device_id_type=MESH)
        for r in range(1, mp_size):
            pl.semaphore_signal(barrier, inc=1, device_id=peer(r), device_id_type=MESH)
        loads = {}
        for name, src, dst in (
            ("tok", tok_hbm, tok), ("q", wq_hbm, wq), ("k", wk_hbm, wk), ("v", wv_hbm, wv),
            ("o", wo_hbm, wo), ("up", up_hbm, wu.at[mp]), ("down", down_hbm, wd.at[mp]), ("cot", cot_hbm, cot),
        ):
            loads[name] = local(src, dst)
            loads[name].start()
        for index, source in enumerate((b_q, b_k, b_v, b_o, g_a, s_a, b_d, g_f, s_f)):
            vec[index : index + 1, :] = source[...].reshape(1, width)
        vec[15:16, :] = b_u[...].reshape(1, shard)
        ub[mp] = jnp.broadcast_to(vec[15:16, :], (8, shard))
        def w_base(kind, upto):
            bits = w_order(kind)
            base = 0
            for s in range(nhalf - 1, upto - 1, -1):
                base = base + bit(bits[s]) * (piece << s)
            return base

        half_cols = shard // 2

        def weight_job(kind, i, side):
            source, buf = ((up_hbm, wu), (down_hbm, wd))[kind]
            cols_at = pl.ds(side * half_cols, half_cols)
            at = rds(w_base(side, 0), piece)
            copy = remote(source.at[at, cols_at], buf.at[mp, at, cols_at], {"mp": across(i)})
            copy.start()
            yield
            for s in range(nhalf):
                copy.wait()
                ref = buf.at[across(i), rds(w_base(side, s), piece << s), cols_at]
                copy = remote(ref, ref, flip(w_order(side)[s]))
                copy.start()
                yield
            copy.wait()
            yield

        weight_jobs = {
            (kind, i, side): weight_job(kind, i, side)
            for kind in (0, 1) for i in range(1, mp_size) for side in (0, 1)
        }

        def pump(kind, which=range(1, mp_size)):
            for i in which:
                for side in (0, 1):
                    next(weight_jobs[kind, i, side])

        own_start = mp * rows

        def layout(places):
            opened = jnp.full(places.shape, 0, jnp.int32) + starts[0, 0]
            closed = jnp.full(places.shape, SEQ, jnp.int32)
            if DOCS > 1:
                closed = jnp.full(places.shape, 0, jnp.int32) + starts[0, 1]
            number = jnp.zeros(places.shape, jnp.int32)
            for d in range(1, DOCS):
                ending = starts[0, d + 1] if d + 1 < DOCS else SEQ
                inside = places >= starts[0, d]
                opened = jnp.where(inside, starts[0, d], opened)
                closed = jnp.where(inside, ending, closed)
                number = number + inside.astype(jnp.int32)
            angles = (places - opened).astype(F32) * (0.5 * math.pi) / (closed - opened).astype(F32)
            return number, jnp.cos(angles), jnp.sin(angles)

        places = own_start + lax.broadcasted_iota(jnp.int32, (rows, 128), 0)
        number_c, cos_c, sin_c = layout(places)
        row_places = own_start + lax.broadcasted_iota(jnp.int32, (8, rows), 1)
        number_r, cos_r, sin_r = layout(row_places)
        edge = jnp.zeros((8, 128), jnp.int32)
        last, _, _ = layout(edge + own_start + (rows - 1))
        before, _, _ = layout(edge + own_start - 1)
        has_prev = jnp.where(edge + mp > 0, 1.0, 0.0)
        carried = jnp.where(number_c == before[:1], 1.0, 0.0) * has_prev[:1]
        in_last = jnp.where(number_c == last[:1], 1.0, 0.0)
        linked = (jnp.where(before == last, 1.0, 0.0) * has_prev)[:1]
        cols[0] = cos_c * carried
        cols[1] = sin_c * carried
        cols[2] = cos_c * in_last
        cols[3] = sin_c * in_last
        linked2 = jnp.concatenate([linked, linked], axis=1)
        linked6 = jnp.concatenate([linked] * (width // 128), axis=1)
        wide = jnp.concatenate([number_c, number_c], axis=1)
        wide_cos = jnp.concatenate([cos_c, cos_c], axis=1)
        wide_sin = jnp.concatenate([sin_c, sin_c], axis=1)
        row_id = lax.broadcasted_iota(jnp.int32, (rows, rows), 0)
        col_id = lax.broadcasted_iota(jnp.int32, (rows, rows), 1)
        angle_gap = wide_cos * cos_r[:1] + wide_sin * sin_r[:1]
        same = wide == number_r[:1]
        lower = jnp.where(same & (col_id <= row_id), angle_gap, 0.0)
        upper_part = jnp.where(same & (col_id >= row_id), angle_gap, 0.0)
        m2[:, :rows] = lower
        m2[:, rows:] = lower
        mt2[:, :rows] = upper_part
        mt2[:, rows:] = upper_part

        lane = lax.broadcasted_iota(jnp.int32, (rows, PAIR), 1)
        low_f = jnp.where(lane < HD, 1.0, 0.0)
        high_f = 1.0 - low_f
        first_two = jnp.where(lax.rem(lane, HD) < 2, 1.0, 0.0)
        o2[:rows, :] = low_f.astype(BF)
        o2[rows:, :] = high_f.astype(BF)
        c1[:rows, :] = (first_two * low_f).astype(BF)
        c1[rows:, :] = (first_two * high_f).astype(BF)
        ec[...] = first_two.astype(BF)
        block_row = lax.broadcasted_iota(jnp.int32, (2 * PAIR, PAIR), 0)
        block_col = lax.broadcasted_iota(jnp.int32, (2 * PAIR, PAIR), 1)
        bb[...] = jnp.where(
            lax.div(lax.rem(block_row, PAIR), HD) == lax.div(block_col, HD), 1.0, 0.0
        ).astype(BF)
        lo = low_f.astype(BF)[:16]
        hi = high_f.astype(BF)[:16]
        masks[0] = lo
        masks[1] = hi
        masks[2] = jnp.where(lax.rem(lane, HD) == 0, 1.0, 0.0).astype(BF)[:16]
        masks[3] = jnp.where(lax.rem(lane, HD) == 1, 1.0, 0.0).astype(BF)[:16]

        def halves(x):
            return jnp.concatenate([x * masks[0, :1], x * masks[1, :1]], axis=0)

        def expand(compact):
            low4 = jnp.concatenate([masks[0, :1]] * 2, axis=1)
            high4 = jnp.concatenate([masks[1, :1]] * 2, axis=1)
            return jnp.concatenate([compact * low4, compact * high4], axis=0)

        def compact_of(full):
            low4 = jnp.concatenate([masks[0, :1]] * 2, axis=1).astype(F32)
            high4 = jnp.concatenate([masks[1, :1]] * 2, axis=1).astype(F32)
            return full[:HD] * low4 + full[HD:] * high4

        def project(weight, out, name, row):
            loads[name].wait()
            for j in range(width // TILE):
                at = pl.ds(j * TILE, TILE)
                y = mm(tok[...], weight[:, at]) + vec[row : row + 1, at]
                if row < 2:
                    y = jnp.maximum(y, 0.0)
                out[:, at] = y.astype(BF)

        loads["tok"].wait()
        project(wk, rk, "k", 1)
        project(wv, vv, "v", 2)

        def lanes(p):
            return pl.ds(pl.multiple_of(p * PAIR, PAIR), PAIR)

        def feats(ref, p, which):
            x = ref[:, lanes(p)].astype(F32)
            return (x * cols[which]).astype(BF), (x * cols[which + 1]).astype(BF)

        def contribs(p, carry):
            kc, ks = feats(rk, p, 2)
            full = mm_tn(vv[:, lanes(p)], jnp.concatenate([kc, ks], axis=1))
            state[p] = compact_of(full)
            ssum[0:1, lanes(p)] = col_sum(kc.astype(F32))
            ssum[1:2, lanes(p)] = col_sum(ks.astype(F32))
            return carry

        ssum[...] = jnp.zeros_like(ssum)
        lax.fori_loop(0, PAIRS, contribs, 0)

        CH = 3
        PC = PAIRS // CH

        class Chain:
            def __init__(self, out_state, out_sum, in_state, in_sum, forward):
                step = 1 if forward else mp_size - 1
                self.has_in = (mp > 0) if forward else (mp < mp_size - 1)
                self.has_out = (mp < mp_size - 1) if forward else (mp > 0)
                self.rank = mp if forward else mp_size - 1 - mp
                self.refs = out_state, out_sum, in_state, in_sum
                self.copies = [
                    remote(out_state.at[pl.ds(c * PC, PC)], in_state.at[pl.ds(c * PC, PC)], peer(step))
                    for c in range(CH)
                ]
                self.sum_copy = remote(out_sum, in_sum, peer(step))

            def early(self):
                out_state, out_sum, in_state, in_sum = self.refs

                @pl.when(jnp.logical_not(self.has_in))
                def _():
                    in_state[...] = jnp.zeros_like(in_state)
                    in_sum[...] = jnp.zeros_like(in_sum)
                    out_sum[...] = ssum[...]
                    self.sum_copy.start()
                    for c in range(CH):
                        at = pl.ds(c * PC, PC)
                        out_state[at] = state[at].astype(BF)
                        self.copies[c].start()

            def slot(self, k):
                for c in range(CH):
                    if 0 <= k - c <= mp_size - 2:
                        self.service(c, self.rank == k - c + 1)

            def service(self, c, here):
                out_state, out_sum, in_state, in_sum = self.refs

                @pl.when(here)
                def _():
                    if c == 0:
                        self.sum_copy.wait_recv()

                        @pl.when(self.has_out)
                        def _():
                            out_sum[...] = ssum[...] + in_sum[...] * linked6
                            self.sum_copy.start()

                    self.copies[c].wait_recv()

                    @pl.when(self.has_out)
                    def _():
                        for p in range(c * PC, (c + 1) * PC):
                            out_state[p] = (state[p] + in_state[p].astype(F32) * linked2).astype(BF)
                        self.copies[c].start()

            def finish(self):
                @pl.when(self.has_out)
                def _():
                    for copy in self.copies + [self.sum_copy]:
                        copy.wait_send()

        ahead = Chain(state_out, ssum_out, state_in, ssum_in, True)
        behind = Chain(state_out, gsum_out, grad_in, gsum_in, False)
        neighbour = {"mp": across(1)}
        norm_pair = remote(nf.at[pl.ds(0, rows)], nf.at[pl.ds(rows, rows)], neighbour)
        merged_pair = remote(mf.at[pl.ds(0, rows)], mf.at[pl.ds(rows, rows)], neighbour)
        pl.semaphore_wait(barrier, nbits + mp_size - 1)
        pump(0, [1, 2])
        ahead.early()
        bias_copies = [remote(ub.at[mp], ub.at[mp], {"mp": across(i)}) for i in range(1, mp_size)]
        for copy in bias_copies:
            copy.start()
        project(wq, rq, "q", 0)
        flow = [(k, i) for k in (0, 1) for i in range(1, mp_size)]

        def wave(d):
            for stage in range(nhalf + 1):
                if 0 <= d - stage < len(flow):
                    kind, i = flow[d - stage]
                    pump(kind, [i])

        def local_attention(p, carry):
            k2 = halves(rk[:, lanes(p)])
            a = (mm_nt(rq[:, lanes(p)], k2) * m2[...]).astype(BF)
            both = mm(a, jnp.concatenate([halves(vv[:, lanes(p)]), o2[...]], axis=1))
            num[:, lanes(p)] = both[:, :PAIR]
            den[:, lanes(p)] = both[:, PAIR:]
            return carry

        for c in range(CH):
            lax.fori_loop(c * PC, (c + 1) * PC, local_attention, 0)
            wave(c)
            pump(0, [3]) if c == 0 else pump(1, [c])
            ahead.slot(c)
        wave(3)
        pump(1, [3])
        ahead.slot(3)
        wave(4)
        ahead.slot(4)

        def remote_attention(p, carry):
            at = lanes(p)
            qc, qs = feats(rq, p, 0)
            carry_num = mm_nt(jnp.concatenate([qc, qs], axis=1), expand(state_in[p]))
            weighted = qc.astype(F32) * ssum_in[0:1, at] + qs.astype(F32) * ssum_in[1:2, at]
            total = den[:, at] + mm(two_parts(weighted), bb[...])
            value = (num[:, at] + carry_num) / jnp.maximum(total, 1.0)
            den[:, at] = total
            num[:, at] = value
            ctx[:, at] = value.astype(BF)
            return carry

        lax.fori_loop(0, PAIRS, remote_attention, 0)

        loads["o"].wait()
        for j in range(width // TILE):
            at = pl.ds(j * TILE, TILE)
            hid[:, at] = tok[:, at].astype(F32) + mm(ctx[...], wo[:, at]) + vec[3:4, at]
        RB = 64

        def first_norm(i, carry):
            at = pl.ds(pl.multiple_of(i * RB, RB), RB)
            x = hid[at, :]
            center = x - jnp.mean(x, axis=1, keepdims=True)
            inv = lax.rsqrt(jnp.mean(center * center, axis=1, keepdims=True) + 1e-05)
            xhat = center * inv
            y = xhat * vec[4:5, :] + vec[5:6, :]
            hid[at, :] = xhat
            rstd[at, :] = jnp.broadcast_to(inv, (RB, 128))
            normed[at, :] = y
            nf[at, :] = y.astype(BF)
            return carry

        lax.fori_loop(0, rows // RB, first_norm, 0)
        norm_pair.start()

        def ffn_up(t):
            for j in range(shard // TILE):
                at = pl.ds(j * TILE, TILE)
                u = mm(nf[:rows, :], wu[t, :, at]) + ub[t, 0:1, at]
                value, slope = gelu_both(u)
                acted[t, :, at] = value.astype(BF)
                gps[t, :, at] = slope

        def ffn_down(t, first):
            for j in range(width // TILE):
                at = pl.ds(j * TILE, TILE)
                y = mm(acted[t], wd[t, :, at])
                if first:
                    acc[:, at] = y
                else:
                    acc[:, at] += y

        loads["up"].wait()
        loads["down"].wait()
        for copy in bias_copies:
            copy.wait()
        ffn_up(mp)
        wave(5)
        ffn_up(across(1))
        ffn_up(across(2))
        ffn_up(across(3))
        ffn_down(mp, True)
        wave(6)
        ffn_down(across(1), False)
        wave(7)
        ffn_down(across(2), False)
        wave(8)
        ffn_down(across(3), False)
        small[0] = jnp.zeros_like(small[0])
        loads["cot"].wait()

        def second_norm(i, carry):
            at = pl.ds(pl.multiple_of(i * RB, RB), RB)
            x = normed[at, :] + acc[at, :] + vec[6:7, :]
            center = x - jnp.mean(x, axis=1, keepdims=True)
            inv = lax.rsqrt(jnp.mean(center * center, axis=1, keepdims=True) + 1e-05)
            xhat = center * inv
            in_out[0, at, :] = (xhat * vec[7:8, :] + vec[8:9, :]).astype(BF)
            g = cot[at, :].astype(F32)
            s = g * vec[7:8, :]
            grad = (
                s - jnp.mean(s, axis=1, keepdims=True) - xhat * jnp.mean(s * xhat, axis=1, keepdims=True)
            ) * inv
            mg[at, :] = grad
            mf[at, :] = grad.astype(BF)
            small[0, 7:8, :] += col_sum(g * xhat)
            small[0, 8:9, :] += col_sum(g)
            small[0, 6:7, :] += col_sum(grad)
            return carry

        lax.fori_loop(0, rows // RB, second_norm, 0)
        layer_copy = local(in_out.at[0], out_layer)
        layer_copy.start()
        merged_pair.start()

        def ffn_back(r, carry):
            t = lax.rem(mp + r, mp_size)
            for j in range(shard // TILE):
                at = pl.ds(j * TILE, TILE)
                up_grad = mm_nt(mf[:rows, :], wd[t, at, :]) * gps[t, :, at]
                upl2[:rows, at] = up_grad.astype(BF)
            for j in range(width // TILE):
                at = pl.ds(j * TILE, TILE)
                mg[:, at] += mm_nt(upl2[:rows, :], wu[t, at, :])
            return carry

        lax.fori_loop(0, mp_size, ffn_back, 0)

        def norm_back(i, carry):
            at = pl.ds(pl.multiple_of(i * RB, RB), RB)
            g = mg[at, :]
            xhat = hid[at, :]
            s = g * vec[4:5, :]
            inv = rstd[at, 0:1]
            grad = (
                s - jnp.mean(s, axis=1, keepdims=True) - xhat * jnp.mean(s * xhat, axis=1, keepdims=True)
            ) * inv
            acc[at, :] = grad
            hlow[at, :] = grad.astype(BF)
            small[0, 4:5, :] += col_sum(g * xhat)
            small[0, 5:6, :] += col_sum(g)
            small[0, 3:4, :] += col_sum(grad)
            return carry

        lax.fori_loop(0, rows // RB, norm_back, 0)
        for j in range(width // TILE):
            at = pl.ds(j * TILE, TILE)
            gv[:, at] = mm_nt(hlow[...], wo[at, :]).astype(BF)

        def back_state(p, carry):
            at = lanes(p)
            total = den[:, at]
            inv = 1.0 / jnp.maximum(total, 1.0)
            g = gv[:, at].astype(F32)
            numer = (g * inv).astype(BF)
            sums = mm(two_parts(g * num[:, at]), bb[...])
            den_grad = jnp.where(total > 1.0, -sums * inv, 0.0)
            ngr[:, at] = numer
            mg[:, at] = den_grad
            qc, qs = feats(rq, p, 0)
            full = mm_tn(numer, jnp.concatenate([qc, qs], axis=1))
            state[p] = compact_of(full)
            ssum[0:1, at] = col_sum(qc.astype(F32) * den_grad)
            ssum[1:2, at] = col_sum(qs.astype(F32) * den_grad)
            return carry

        ssum[...] = jnp.zeros_like(ssum)
        ahead.finish()
        lax.fori_loop(0, PAIRS, back_state, 0)
        behind.early()

        def weight_grad(index, left_t, right):
            def body(i, carry):
                at = rds(i * TILE, TILE, TILE)
                for j in range(width // TILE):
                    to = pl.ds(j * TILE, TILE)
                    part[rds(index * width + i * TILE, TILE, TILE), to] = mm(
                        left_t[at, :], right[:, to]
                    ).astype(BF)
                return carry

            lax.fori_loop(0, width // TILE, body, 0)


        def j_base(job, upto):
            base = 0
            for s in range(upto):
                base = base + bit(jobs[job][s]) * (width >> (s + 1))
            return base

        reds = [red0, red1, red2]

        def part_of(job):
            if job < 4:
                return part.at[pl.ds(job * width, width)]
            return (wu, wd)[job % 2].at[across((1, 3)[(job - 4) // 2])]

        def add_rows(ref, start, count, received):
            step = min(count, 96)

            def body(i, carry):
                at = rds(start + i * step, step)
                ref[at, :] = (
                    ref[at, :].astype(F32) + received[rds(i * step, step), :].astype(F32)
                ).astype(BF)
                return carry

            lax.fori_loop(0, count // step, body, 0)

        def scatter_job(job):
            ref = part_of(job)
            for s in range(nhalf):
                half = width >> (s + 1)
                b = jobs[job][s]
                away = j_base(job, s) + (1 - bit(b)) * half
                copy = remote(ref.at[rds(away, half)], reds[s].at[job], flip(b))
                copy.start()
                yield
                copy.wait()
                add_rows(ref, j_base(job, s + 1), half, reds[s].at[job])
            for e, b in enumerate(range(nhalf, nbits)):
                at = rds(j_base(job, nhalf), piece)
                copy = remote(ref.at[at], redx.at[job, e], flip(b))
                copy.start()
                copy.wait()
                add_rows(ref, j_base(job, nhalf), piece, redx.at[job, e])
            yield

        outs = [out_q, out_o, out_v, out_k, out_up, out_down]
        final_copies = []

        def gather_job(job):
            for s in range(nhalf - 1, -1, -1):
                at = rds(job * width + j_base(job, s + 1), width >> (s + 1))
                copy = remote(gsum.at[at], gsum.at[at], flip(jobs[job][s]))
                copy.start()
                yield
                copy.wait()
            out = local(gsum.at[pl.ds(job * width, width)], outs[job])
            out.start()
            final_copies.append(out)
            yield

        quarter = piece // 2

        def quarter_row(first, t):
            which = lax.div(t, 2)
            base = (1 - which) * j_base(first, nhalf) + which * j_base(first + 1, nhalf)
            return (first + which) * width + base + lax.rem(t, 2) * quarter

        def z_job(first, slot):
            copies = []
            for i in range(1, mp_size):
                copies.append(
                    remote(
                        part.at[rds(quarter_row(first, across(i)), quarter)],
                        zr.at[slot, i - 1], {"mp": across(i)},
                    )
                )
                copies[-1].start()
            yield
            for copy in copies:
                copy.wait()
            at = rds(quarter_row(first, mp), quarter)
            total = part[at, :].astype(F32)
            for i in range(mp_size - 1):
                total = total + zr[slot, i].astype(F32)
            gsum[at, :] = total.astype(BF)
            copies = [remote(gsum.at[at], gsum.at[at], {"mp": across(i)}) for i in range(1, mp_size)]
            for copy in copies:
                copy.start()
            yield
            for copy in copies:
                copy.wait()
            yield

        def small_job():
            for b in range(nbits):
                copy = remote(small.at[b], smallr.at[b], flip(b))
                copy.start()
                yield
                copy.wait()
                small[b + 1] = small[b] + smallr[b]
            smallz[mp] = small[nbits]
            copies = [remote(smallz.at[mp], smallz.at[mp], {"mp": across(i)}) for i in range(1, mp_size)]
            for copy in copies:
                copy.start()
            yield
            for copy in copies:
                copy.wait()
            total = smallz[0]
            for z in range(1, mp_size):
                total = total + smallz[z]
            smallr[0, 0:8] = total[0:8]
            smallr[0, 8:16] = total[8:16]
            smallr[0, 15:16] = smallz[mp, 15:16] + smallz[across(2), 14:15]
            out = local(smallr.at[0], out_small)
            out.start()
            final_copies.append(out)
            yield

        def ff_z_job():
            copies = []
            for slot, job in enumerate((UB, DB)):
                at = rds(j_base(job, nhalf), piece)
                copies.append(remote(part_of(job).at[at], zf.at[slot], {"mp": across(2)}))
                copies[-1].start()
            yield
            for copy in copies:
                copy.wait()
            for slot, job in enumerate((UA, DA)):
                total = part_of(job)[rds(j_base(job, nhalf), piece), :].astype(F32) + zf[slot].astype(F32)
                gsum[rds(job * width + j_base(job, nhalf), piece), :] = total.astype(BF)
            yield

        Q, O, V, K, UA, DA, UB, DB = range(8)
        ff_z = ff_z_job()
        scatter = [scatter_job(job) for job in range(8)]
        gather = [gather_job(job) for job in range(6)]
        z_first = z_job(Q, 0)
        z_second = z_job(V, 1)
        smalls = small_job()

        def step(*generators):
            for g in generators:
                assert next(g, 1) is None

        tokt[...] = ctx[...].T
        weight_grad(O, tokt, hlow)
        step(scatter[O])

        def back_local(p, carry):
            at = lanes(p)
            qp = rq[:, at]
            kp = rk[:, at]
            vp = vv[:, at]
            numer = ngr[:, at]
            den_grad = mg[:, at]
            k2 = halves(kp)
            q2 = halves(qp)
            n2 = halves(numer)
            dh = den_grad.astype(BF)
            dl = (den_grad - dh.astype(F32)).astype(BF)
            x = dh * masks[2, :1] + dl * masks[3, :1]
            ds = (
                mm_nt(
                    jnp.concatenate([numer, x], axis=1),
                    jnp.concatenate([halves(vp), c1[...]], axis=1),
                )
                * m2[...]
            ).astype(BF)
            grad_q = mm(ds, k2)
            at_scores = (mm_nt(kp, q2) * mt2[...]).astype(BF)
            gv_part = mm(at_scores, n2)
            dst = (
                mm_nt(
                    jnp.concatenate([vp, ec[...]], axis=1),
                    jnp.concatenate([n2, halves(x)], axis=1),
                )
                * mt2[...]
            ).astype(BF)
            gk_part = mm(dst, q2)
            t = mm(numer, expand(state_in[p]))
            cq = cols[0]
            sq = cols[1]
            grad_q = grad_q + cq * t[:, :PAIR] + sq * t[:, PAIR:]
            grad_q = grad_q + den_grad * (cq * ssum_in[0:1, at] + sq * ssum_in[1:2, at])
            grad_q = jnp.where(qp.astype(F32) > 0.0, grad_q, 0.0)
            small[0, 0:1, at] = col_sum(grad_q)
            gq[:, at] = grad_q.astype(BF)
            normed[:, at] = gk_part
            hid[:, at] = gv_part
            return carry

        for c in range(CH):
            lax.fori_loop(c * PC, (c + 1) * PC, back_local, 0)
            if c == 0:
                step(scatter[O])
            behind.slot(c)
        behind.slot(3)
        behind.slot(4)
        tokt[...] = tok[...].T
        weight_grad(Q, tokt, gq)
        step(scatter[Q])

        def back_remote(p, carry):
            at = lanes(p)
            full = expand(grad_in[p])
            t = mm(vv[:, at], full)
            kc, ks = feats(rk, p, 2)
            ck = cols[2]
            sk = cols[3]
            grad_k = normed[:, at] + ck * (t[:, :PAIR] + gsum_in[0:1, at]) + sk * (
                t[:, PAIR:] + gsum_in[1:2, at]
            )
            grad_k = jnp.where(rk[:, at].astype(F32) > 0.0, grad_k, 0.0)
            small[0, 1:2, at] = col_sum(grad_k)
            gk[:, at] = grad_k.astype(BF)
            grad_v = hid[:, at] + mm_nt(jnp.concatenate([kc, ks], axis=1), full)
            small[0, 2:3, at] = col_sum(grad_v)
            gv[:, at] = grad_v.astype(BF)
            return carry

        lax.fori_loop(0, PAIRS, back_remote, 0)
        weight_grad(K, tokt, gk)
        step(scatter[K])
        weight_grad(V, tokt, gv)
        step(scatter[V], scatter[Q], scatter[O], scatter[K])

        for j in range(width // TILE):
            at = pl.ds(j * TILE, TILE)
            total = acc[:, at] + mm_nt(gq[...], wq[at, :]) + mm_nt(gk[...], wk[at, :])
            in_out[1, :, at] = (total + mm_nt(gv[...], wv[at, :])).astype(BF)
        input_copy = local(in_out.at[1], out_input)
        input_copy.start()
        step(scatter[V], scatter[Q], scatter[O])

        norm_pair.wait()
        merged_pair.wait()

        def shard_grads(t, up_job, down_job, row):
            for j in range(shard // TILE):
                at = pl.ds(j * TILE, TILE)
                u = mm(nf[...], wu[t, :, at]) + ub[t, 0:1, at]
                value, slope = gelu_both(u)
                up_grad = mm_nt(mf[...], wd[t, at, :]) * slope
                small[0, row : row + 1, at] = col_sum(up_grad)
                act2[:, at] = value.astype(BF)
                upl2[:, at] = up_grad.astype(BF)
            for j in range(width // TILE):
                at = pl.ds(j * TILE, TILE)
                part_of(up_job)[pl.ds(j * TILE, TILE), :] = mm_tn(nf[:, at], upl2[...]).astype(BF)
            for j in range(shard // TILE):
                at = pl.ds(j * TILE, TILE)
                part_of(down_job)[pl.ds(j * TILE, TILE), :] = mm_tn(act2[:, at], mf[...]).astype(BF)

        shard_grads(across(2), UB, DB, 14)
        step(scatter[UB], scatter[DB])
        step(scatter[Q])
        step(z_first, scatter[V], scatter[K])
        shard_grads(mp, UA, DA, 15)
        step(scatter[UA], scatter[DA], smalls)
        step(z_first)
        step(scatter[UB], scatter[DB])
        step(scatter[V], scatter[K], z_second)
        step(scatter[UA], scatter[DA], smalls)
        step(z_first, gather[Q], gather[O])
        step(scatter[UB], scatter[DB], z_second)
        step(scatter[UA], scatter[DA], smalls)
        step(gather[Q], gather[O])
        step(z_second, gather[V], gather[K])
        step(scatter[UB], scatter[DB], ff_z)
        step(gather[Q], gather[O], smalls)
        step(gather[V], gather[K])
        step(scatter[UA], scatter[DA], ff_z, gather[UA], gather[DA])
        step(gather[Q], gather[O])
        step(gather[V], gather[K], smalls)
        step(gather[UA], gather[DA])
        step(gather[V], gather[K])
        step(gather[UA], gather[DA])
        step(gather[UA], gather[DA])
        for _ in smalls:
            pass
        for g in scatter + gather + [z_first, z_second, ff_z, smalls] + list(weight_jobs.values()):
            assert next(g, 1) == 1
        behind.finish()
        layer_copy.wait()
        input_copy.wait()
        for copy in final_copies:
            copy.wait()

    def call(*operands):
        vm = pltpu.VMEM
        big = lambda *s: vm(s, BF)
        flt = lambda *s: vm(s, F32)
        nsem = 224
        square = jax.ShapeDtypeStruct((width, width), BF)
        scratch = [
            big(rows, width), big(rows, width), big(width, width), big(width, width), big(width, width),
            big(width, width), flt(16, width),
            big(mp_size, width, shard), big(mp_size, shard, width), flt(mp_size, 8, shard),
            big(rows, width), big(rows, width), big(rows, width),
            flt(rows, 2 * rows), flt(rows, 2 * rows), flt(4, rows, 128),
            big(2 * rows, PAIR), big(2 * PAIR, PAIR), big(2 * rows, PAIR), big(rows, PAIR), big(4, 16, PAIR),
            flt(PAIRS, HD, 2 * PAIR), big(PAIRS, HD, 2 * PAIR), flt(8, width), flt(8, width),
            big(PAIRS, HD, 2 * PAIR), flt(8, width), big(PAIRS, HD, 2 * PAIR), flt(8, width),
            flt(8, width),
            flt(rows, width), flt(rows, width), big(rows, width), flt(rows, width), flt(rows, 128),
            flt(rows, width), big(2 * rows, width), big(2 * rows, width),
            big(mp_size, rows, shard), flt(mp_size, rows, shard), big(2 * rows, shard), big(2 * rows, shard),
            big(2, piece, width), flt(rows, width), flt(rows, width),
            big(rows, width), big(rows, width),
            big(rows, width), big(rows, width), big(rows, width),
            big(4 * width, width), big(6 * width, width),
            big(8, width // 2, width), big(8, width // 4, width), big(8, width // 8, width),
            big(8, max(1, nbits - nhalf), 16 if nbits == nhalf else piece, width), big(2, mp_size - 1, piece // 2, width),
            flt(nbits + 1, 16, width), flt(nbits, 16, width), flt(mp_size, 16, width),
            big(width, rows), big(2, rows, width),
            pltpu.SemaphoreType.DMA((32,)), pltpu.SemaphoreType.DMA((nsem,)), pltpu.SemaphoreType.DMA((nsem,)),
        ]
        spec = pl.BlockSpec(memory_space=pltpu.VMEM)
        anywhere = pl.BlockSpec(memory_space=pl.ANY)
        return pl.pallas_call(
            kernel,
            out_shape=(
                jax.ShapeDtypeStruct((rows, width), BF),
                jax.ShapeDtypeStruct((rows, width), BF),
                square, square, square, square, square, square,
                jax.ShapeDtypeStruct((16, width), F32),
            ),
            in_specs=[pl.BlockSpec(memory_space=pltpu.SMEM)] + [spec] * 10 + [anywhere] * 8,
            out_specs=(anywhere,) * 9,
            scratch_shapes=scratch,
            compiler_params=pltpu.CompilerParams(
                collective_id=0, has_side_effects=True, vmem_limit_bytes=63 * 1024 * 1024
            ),
        )(*operands)

    return call


def widen(layer, back, grads, small):
    rows, width = layer.shape
    steps = 2

    def kernel(*refs):
        n = len(grads)
        ins, outs = refs[: n + 3], refs[n + 3 :]
        outs[0][...] = ins[0][...]
        outs[1][...] = ins[1][...]
        for g in range(n):
            outs[2 + g][...] = ins[2 + g][...].astype(F32)

        @pl.when(pl.program_id(0) == 0)
        def _():
            for row, out in zip((0, 1, 2, 3, 4, 5, 15, 6, 7, 8), outs[2 + n :]):
                out[...] = ins[2 + n][row : row + 1, :].reshape(width)

    block = lambda x: pl.BlockSpec((x.shape[0] // steps, x.shape[1]), lambda i: (i, 0))
    whole = pl.BlockSpec(small.shape, lambda i: (0, 0))
    vector = pl.BlockSpec((width,), lambda i: (0,))
    mats = [layer, back, *grads]
    return pl.pallas_call(
        kernel,
        grid=(steps,),
        in_specs=[block(x) for x in mats] + [whole],
        out_specs=[block(x) for x in mats] + [vector] * 10,
        out_shape=[jax.ShapeDtypeStruct(x.shape, BF) for x in (layer, back)]
        + [jax.ShapeDtypeStruct(x.shape, F32) for x in grads]
        + [jax.ShapeDtypeStruct((width,), F32)] * 10,
        compiler_params=pltpu.CompilerParams(vmem_limit_bytes=62 * 1024 * 1024),
    )(*mats, small)


def solution(mesh):
    dp_size, mp_size = mesh.shape["dp"], mesh.shape["mp"]

    def on_device(
        tokens, doc_starts, query_proj, key_proj, value_proj, query_bias, key_bias, value_bias,
        output_proj, output_bias, attn_gain, attn_shift, up_proj, up_bias, down_proj, down_bias,
        ffn_gain, ffn_shift, cotangent,
    ):
        _, rows, width = tokens.shape
        shard = up_proj.shape[1]
        call = build(dp_size, mp_size, rows, width, shard)
        layer_out, input_grad, gq, gk, gv, go, gu, gd, small = call(
            doc_starts, query_bias, key_bias, value_bias, output_bias, attn_gain, attn_shift,
            down_bias, ffn_gain, ffn_shift, up_bias, tokens[0], cotangent[0],
            query_proj, key_proj, value_proj, output_proj, up_proj, down_proj,
        )
        layer_out, input_grad, gq, gk, gv, go, gu, gd, *vecs = widen(
            layer_out, input_grad, (gq, gk, gv, go, gu, gd), small
        )
        bq, bk, bv, bo, ga, sa, bu, bd, gf, sf = vecs
        return (
            layer_out[None], input_grad[None], gq, gk, gv, bq, bk, bv, go, bo, ga, sa,
            gu, bu, gd, bd, gf, sf,
        )

    rows_spec = P("dp", "mp", None)
    placed = (
        rows_spec, P("dp", None), P(), P(), P(), P(), P(), P(), P(), P(), P(), P(),
        P(None, "mp"), P("mp"), P("mp", None), P(), P(), P(), rows_spec,
    )
    results = (
        rows_spec, rows_spec, P(), P(), P(), P(), P(), P(), P(), P(), P(), P(),
        P(None, "mp"), P("mp"), P("mp", None), P(), P(), P(),
    )
    return jax.shard_map(
        on_device, mesh=mesh, in_specs=placed, out_specs=results, check_vma=False
    )
```

```python
import math

import jax
import jax.numpy as jnp
from jax import lax
from jax.experimental import pallas as pl
from jax.experimental.pallas import tpu as pltpu
from jax.sharding import PartitionSpec as P

HEADS = 12
HD = 64
SEQ = 1024
DOCS = 2
PAIR = 2 * HD
PAIRS = HEADS // 2
TILE = 256
MESH = pl.DeviceIdType.MESH
BF = jnp.bfloat16
F32 = jnp.float32
C0 = math.sqrt(2.0 / math.pi)
C1 = 0.044715


def mm(a, b):
    return lax.dot_general(a, b, (((1,), (0,)), ((), ())), preferred_element_type=F32)


def mm_nt(a, b):
    return lax.dot_general(a, b, (((1,), (1,)), ((), ())), preferred_element_type=F32)


def mm_tn(a, b):
    return lax.dot_general(a, b, (((0,), (0,)), ((), ())), preferred_element_type=F32)


def gelu_both(u):
    square = u * u
    t = jnp.tanh(C0 * u * (1.0 + C1 * square))
    half = 0.5 * (1.0 + t)
    slope = half + (0.5 * C0) * u * (1.0 - t * t) * (1.0 + (3.0 * C1) * square)
    return u * half, slope


def two_parts(x):
    high = x.astype(BF)
    return jnp.concatenate([high, (x - high.astype(F32)).astype(BF)], axis=1)


def col_sum(x):
    return jnp.sum(x, axis=0, keepdims=True)


def build(dp_size, mp_size, rows, width, shard):
    nbits = dp_size.bit_length() - 1
    nhalf = min(3, nbits)
    piece = width >> nhalf

    def order(kind):
        first = list(range(nhalf))
        if kind == 1 and nhalf == 3:
            first = [0, 2, 1]
        return first

    def w_order(kind):
        plain = order(kind)
        return plain[1:] + plain[:1]

    jobs = [order(k % 2) for k in range(8)]

    def kernel(
        starts, b_q, b_k, b_v, b_o, g_a, s_a, b_d, g_f, s_f, b_u,
        tok_hbm, cot_hbm, wq_hbm, wk_hbm, wv_hbm, wo_hbm, up_hbm, down_hbm,
        out_layer, out_input, out_q, out_k, out_v, out_o, out_up, out_down, out_small,
        tok, cot, wq, wk, wv, wo, vec, wu, wd, ub, rq, rk, vv, m2, mt2, cols, o2, bb, c1, ec, masks,
        state, state_in, ssum, ssum_in, grad_in, gsum_in, state_out, ssum_out, gsum_out,
        num, den, ctx, hid, rstd, normed, nf, mf, acted, gps, act2, upl2, zf, acc, mg, hlow, ngr,
        gq, gk, gv, part, gsum, red0, red1, red2, redx, zr, small, smallr, smallz, tokt, in_out,
        local_sem, send_sem, recv_sem,
    ):
        dp = lax.axis_index("dp")
        mp = lax.axis_index("mp")
        counter = [0]
        locals_used = [0]

        def bit(b):
            return lax.rem(lax.div(dp, 1 << b), 2)

        def flip(b):
            return {"dp": dp + (1 - 2 * bit(b)) * (1 << b)}

        def peer(r):
            return {"mp": lax.rem(mp + r, mp_size)}

        def across(i):
            other, span = mp, 1
            while span < mp_size:
                if i & span:
                    other = other + span * (1 - 2 * lax.rem(lax.div(mp, span), 2))
                span *= 2
            return other

        def remote(src, dst, device):
            i = counter[0]
            counter[0] += 1
            return pltpu.make_async_remote_copy(
                src_ref=src, dst_ref=dst, send_sem=send_sem.at[i], recv_sem=recv_sem.at[i],
                device_id=device, device_id_type=MESH,
            )

        def local(src, dst):
            i = locals_used[0]
            locals_used[0] += 1
            return pltpu.make_async_copy(src, dst, local_sem.at[i])

        def rds(start, size, unit=16):
            return pl.ds(pl.multiple_of(start, unit), size)

        barrier = pltpu.get_barrier_semaphore()
        for b in range(nbits):
            pl.semaphore_signal(barrier, inc=1, device_id=flip(b), device_id_type=MESH)
        for r in range(1, mp_size):
            pl.semaphore_signal(barrier, inc=1, device_id=peer(r), device_id_type=MESH)
        loads = {}
        for name, src, dst in (
            ("tok", tok_hbm, tok), ("q", wq_hbm, wq), ("k", wk_hbm, wk), ("v", wv_hbm, wv),
            ("o", wo_hbm, wo), ("up", up_hbm, wu.at[mp]), ("down", down_hbm, wd.at[mp]), ("cot", cot_hbm, cot),
        ):
            loads[name] = local(src, dst)
            loads[name].start()
        for index, source in enumerate((b_q, b_k, b_v, b_o, g_a, s_a, b_d, g_f, s_f)):
            vec[index : index + 1, :] = source[...].reshape(1, width)
        vec[15:16, :] = b_u[...].reshape(1, shard)
        ub[mp] = jnp.broadcast_to(vec[15:16, :], (8, shard))
        def w_base(kind, upto):
            bits = w_order(kind)
            base = 0
            for s in range(nhalf - 1, upto - 1, -1):
                base = base + bit(bits[s]) * (piece << s)
            return base

        half_cols = shard // 2

        def weight_job(kind, i, side):
            source, buf = ((up_hbm, wu), (down_hbm, wd))[kind]
            cols_at = pl.ds(side * half_cols, half_cols)
            at = rds(w_base(side, 0), piece)
            copy = remote(source.at[at, cols_at], buf.at[mp, at, cols_at], {"mp": across(i)})
            copy.start()
            yield
            for s in range(nhalf):
                copy.wait()
                ref = buf.at[across(i), rds(w_base(side, s), piece << s), cols_at]
                copy = remote(ref, ref, flip(w_order(side)[s]))
                copy.start()
                yield
            copy.wait()
            yield

        weight_jobs = {
            (kind, i, side): weight_job(kind, i, side)
            for kind in (0, 1) for i in range(1, mp_size) for side in (0, 1)
        }

        def pump(kind, which=range(1, mp_size)):
            for i in which:
                for side in (0, 1):
                    next(weight_jobs[kind, i, side])

        own_start = mp * rows

        def layout(places):
            opened = jnp.full(places.shape, 0, jnp.int32) + starts[0, 0]
            closed = jnp.full(places.shape, SEQ, jnp.int32)
            if DOCS > 1:
                closed = jnp.full(places.shape, 0, jnp.int32) + starts[0, 1]
            number = jnp.zeros(places.shape, jnp.int32)
            for d in range(1, DOCS):
                ending = starts[0, d + 1] if d + 1 < DOCS else SEQ
                inside = places >= starts[0, d]
                opened = jnp.where(inside, starts[0, d], opened)
                closed = jnp.where(inside, ending, closed)
                number = number + inside.astype(jnp.int32)
            angles = (places - opened).astype(F32) * (0.5 * math.pi) / (closed - opened).astype(F32)
            return number, jnp.cos(angles), jnp.sin(angles)

        places = own_start + lax.broadcasted_iota(jnp.int32, (rows, 128), 0)
        number_c, cos_c, sin_c = layout(places)
        row_places = own_start + lax.broadcasted_iota(jnp.int32, (8, rows), 1)
        number_r, cos_r, sin_r = layout(row_places)
        edge = jnp.zeros((8, 128), jnp.int32)
        last, _, _ = layout(edge + own_start + (rows - 1))
        before, _, _ = layout(edge + own_start - 1)
        has_prev = jnp.where(edge + mp > 0, 1.0, 0.0)
        carried = jnp.where(number_c == before[:1], 1.0, 0.0) * has_prev[:1]
        in_last = jnp.where(number_c == last[:1], 1.0, 0.0)
        linked = (jnp.where(before == last, 1.0, 0.0) * has_prev)[:1]
        cols[0] = cos_c * carried
        cols[1] = sin_c * carried
        cols[2] = cos_c * in_last
        cols[3] = sin_c * in_last
        linked2 = jnp.concatenate([linked, linked], axis=1)
        linked6 = jnp.concatenate([linked] * (width // 128), axis=1)
        wide = jnp.concatenate([number_c, number_c], axis=1)
        wide_cos = jnp.concatenate([cos_c, cos_c], axis=1)
        wide_sin = jnp.concatenate([sin_c, sin_c], axis=1)
        row_id = lax.broadcasted_iota(jnp.int32, (rows, rows), 0)
        col_id = lax.broadcasted_iota(jnp.int32, (rows, rows), 1)
        angle_gap = wide_cos * cos_r[:1] + wide_sin * sin_r[:1]
        same = wide == number_r[:1]
        lower = jnp.where(same & (col_id <= row_id), angle_gap, 0.0)
        upper_part = jnp.where(same & (col_id >= row_id), angle_gap, 0.0)
        m2[:, :rows] = lower
        m2[:, rows:] = lower
        mt2[:, :rows] = upper_part
        mt2[:, rows:] = upper_part

        lane = lax.broadcasted_iota(jnp.int32, (rows, PAIR), 1)
        low_f = jnp.where(lane < HD, 1.0, 0.0)
        high_f = 1.0 - low_f
        first_two = jnp.where(lax.rem(lane, HD) < 2, 1.0, 0.0)
        o2[:rows, :] = low_f.astype(BF)
        o2[rows:, :] = high_f.astype(BF)
        c1[:rows, :] = (first_two * low_f).astype(BF)
        c1[rows:, :] = (first_two * high_f).astype(BF)
        ec[...] = first_two.astype(BF)
        block_row = lax.broadcasted_iota(jnp.int32, (2 * PAIR, PAIR), 0)
        block_col = lax.broadcasted_iota(jnp.int32, (2 * PAIR, PAIR), 1)
        bb[...] = jnp.where(
            lax.div(lax.rem(block_row, PAIR), HD) == lax.div(block_col, HD), 1.0, 0.0
        ).astype(BF)
        lo = low_f.astype(BF)[:16]
        hi = high_f.astype(BF)[:16]
        masks[0] = lo
        masks[1] = hi
        masks[2] = jnp.where(lax.rem(lane, HD) == 0, 1.0, 0.0).astype(BF)[:16]
        masks[3] = jnp.where(lax.rem(lane, HD) == 1, 1.0, 0.0).astype(BF)[:16]

        def halves(x):
            return jnp.concatenate([x * masks[0, :1], x * masks[1, :1]], axis=0)

        def expand(compact):
            low4 = jnp.concatenate([masks[0, :1]] * 2, axis=1)
            high4 = jnp.concatenate([masks[1, :1]] * 2, axis=1)
            return jnp.concatenate([compact * low4, compact * high4], axis=0)

        def compact_of(full):
            low4 = jnp.concatenate([masks[0, :1]] * 2, axis=1).astype(F32)
            high4 = jnp.concatenate([masks[1, :1]] * 2, axis=1).astype(F32)
            return full[:HD] * low4 + full[HD:] * high4

        def project(weight, out, name, row):
            loads[name].wait()
            for j in range(width // TILE):
                at = pl.ds(j * TILE, TILE)
                y = mm(tok[...], weight[:, at]) + vec[row : row + 1, at]
                if row < 2:
                    y = jnp.maximum(y, 0.0)
                out[:, at] = y.astype(BF)

        loads["tok"].wait()
        project(wk, rk, "k", 1)
        project(wv, vv, "v", 2)

        def lanes(p):
            return pl.ds(pl.multiple_of(p * PAIR, PAIR), PAIR)

        def feats(ref, p, which):
            x = ref[:, lanes(p)].astype(F32)
            return (x * cols[which]).astype(BF), (x * cols[which + 1]).astype(BF)

        def contribs(p, carry):
            kc, ks = feats(rk, p, 2)
            full = mm_tn(vv[:, lanes(p)], jnp.concatenate([kc, ks], axis=1))
            state[p] = compact_of(full)
            ssum[0:1, lanes(p)] = col_sum(kc.astype(F32))
            ssum[1:2, lanes(p)] = col_sum(ks.astype(F32))
            return carry

        ssum[...] = jnp.zeros_like(ssum)
        lax.fori_loop(0, PAIRS, contribs, 0)

        CH = 3
        PC = PAIRS // CH

        class Chain:
            def __init__(self, out_state, out_sum, in_state, in_sum, forward):
                step = 1 if forward else mp_size - 1
                self.has_in = (mp > 0) if forward else (mp < mp_size - 1)
                self.has_out = (mp < mp_size - 1) if forward else (mp > 0)
                self.rank = mp if forward else mp_size - 1 - mp
                self.refs = out_state, out_sum, in_state, in_sum
                self.copies = [
                    remote(out_state.at[pl.ds(c * PC, PC)], in_state.at[pl.ds(c * PC, PC)], peer(step))
                    for c in range(CH)
                ]
                self.sum_copy = remote(out_sum, in_sum, peer(step))

            def early(self):
                out_state, out_sum, in_state, in_sum = self.refs

                @pl.when(jnp.logical_not(self.has_in))
                def _():
                    in_state[...] = jnp.zeros_like(in_state)
                    in_sum[...] = jnp.zeros_like(in_sum)
                    out_sum[...] = ssum[...]
                    self.sum_copy.start()
                    for c in range(CH):
                        at = pl.ds(c * PC, PC)
                        out_state[at] = state[at].astype(BF)
                        self.copies[c].start()

            def slot(self, k):
                for c in range(CH):
                    if 0 <= k - c <= mp_size - 2:
                        self.service(c, self.rank == k - c + 1)

            def service(self, c, here):
                out_state, out_sum, in_state, in_sum = self.refs

                @pl.when(here)
                def _():
                    if c == 0:
                        self.sum_copy.wait_recv()

                        @pl.when(self.has_out)
                        def _():
                            out_sum[...] = ssum[...] + in_sum[...] * linked6
                            self.sum_copy.start()

                    self.copies[c].wait_recv()

                    @pl.when(self.has_out)
                    def _():
                        for p in range(c * PC, (c + 1) * PC):
                            out_state[p] = (state[p] + in_state[p].astype(F32) * linked2).astype(BF)
                        self.copies[c].start()

            def finish(self):
                @pl.when(self.has_out)
                def _():
                    for copy in self.copies + [self.sum_copy]:
                        copy.wait_send()

        ahead = Chain(state_out, ssum_out, state_in, ssum_in, True)
        behind = Chain(state_out, gsum_out, grad_in, gsum_in, False)
        neighbour = {"mp": across(1)}
        norm_pair = remote(nf.at[pl.ds(0, rows)], nf.at[pl.ds(rows, rows)], neighbour)
        merged_pair = remote(mf.at[pl.ds(0, rows)], mf.at[pl.ds(rows, rows)], neighbour)
        pl.semaphore_wait(barrier, nbits + mp_size - 1)
        pump(0, [1, 2])
        ahead.early()
        bias_copies = [remote(ub.at[mp], ub.at[mp], {"mp": across(i)}) for i in range(1, mp_size)]
        for copy in bias_copies:
            copy.start()
        project(wq, rq, "q", 0)
        flow = [(k, i) for k in (0, 1) for i in range(1, mp_size)]

        def wave(d):
            for stage in range(nhalf + 1):
                if 0 <= d - stage < len(flow):
                    kind, i = flow[d - stage]
                    pump(kind, [i])

        def local_attention(p, carry):
            k2 = halves(rk[:, lanes(p)])
            a = (mm_nt(rq[:, lanes(p)], k2) * m2[...]).astype(BF)
            both = mm(a, jnp.concatenate([halves(vv[:, lanes(p)]), o2[...]], axis=1))
            num[:, lanes(p)] = both[:, :PAIR]
            den[:, lanes(p)] = both[:, PAIR:]
            return carry

        for c in range(CH):
            lax.fori_loop(c * PC, (c + 1) * PC, local_attention, 0)
            wave(c)
            pump(0, [3]) if c == 0 else pump(1, [c])
            ahead.slot(c)
        wave(3)
        pump(1, [3])
        ahead.slot(3)
        wave(4)
        ahead.slot(4)

        def remote_attention(p, carry):
            at = lanes(p)
            qc, qs = feats(rq, p, 0)
            carry_num = mm_nt(jnp.concatenate([qc, qs], axis=1), expand(state_in[p]))
            weighted = qc.astype(F32) * ssum_in[0:1, at] + qs.astype(F32) * ssum_in[1:2, at]
            total = den[:, at] + mm(two_parts(weighted), bb[...])
            value = (num[:, at] + carry_num) / jnp.maximum(total, 1.0)
            den[:, at] = total
            num[:, at] = value
            ctx[:, at] = value.astype(BF)
            return carry

        lax.fori_loop(0, PAIRS, remote_attention, 0)

        loads["o"].wait()
        for j in range(width // TILE):
            at = pl.ds(j * TILE, TILE)
            hid[:, at] = tok[:, at].astype(F32) + mm(ctx[...], wo[:, at]) + vec[3:4, at]
        RB = 128

        def first_norm(i, carry):
            at = pl.ds(pl.multiple_of(i * RB, RB), RB)
            x = hid[at, :]
            center = x - jnp.mean(x, axis=1, keepdims=True)
            inv = lax.rsqrt(jnp.mean(center * center, axis=1, keepdims=True) + 1e-05)
            xhat = center * inv
            y = xhat * vec[4:5, :] + vec[5:6, :]
            hid[at, :] = xhat
            rstd[at, :] = jnp.broadcast_to(inv, (RB, 128))
            normed[at, :] = y
            nf[at, :] = y.astype(BF)
            return carry

        lax.fori_loop(0, rows // RB, first_norm, 0)
        norm_pair.start()

        def ffn_up(t):
            for j in range(shard // TILE):
                at = pl.ds(j * TILE, TILE)
                u = mm(nf[:rows, :], wu[t, :, at]) + ub[t, 0:1, at]
                value, slope = gelu_both(u)
                acted[t, :, at] = value.astype(BF)
                gps[t, :, at] = slope

        def ffn_down(t, first):
            for j in range(width // TILE):
                at = pl.ds(j * TILE, TILE)
                y = mm(acted[t], wd[t, :, at])
                if first:
                    acc[:, at] = y
                else:
                    acc[:, at] += y

        loads["up"].wait()
        loads["down"].wait()
        for copy in bias_copies:
            copy.wait()
        ffn_up(mp)
        wave(5)
        ffn_up(across(1))
        ffn_up(across(2))
        ffn_up(across(3))
        ffn_down(mp, True)
        wave(6)
        ffn_down(across(1), False)
        wave(7)
        ffn_down(across(2), False)
        wave(8)
        ffn_down(across(3), False)
        small[0] = jnp.zeros_like(small[0])
        loads["cot"].wait()

        def second_norm(i, carry):
            at = pl.ds(pl.multiple_of(i * RB, RB), RB)
            x = normed[at, :] + acc[at, :] + vec[6:7, :]
            center = x - jnp.mean(x, axis=1, keepdims=True)
            inv = lax.rsqrt(jnp.mean(center * center, axis=1, keepdims=True) + 1e-05)
            xhat = center * inv
            in_out[0, at, :] = (xhat * vec[7:8, :] + vec[8:9, :]).astype(BF)
            g = cot[at, :].astype(F32)
            s = g * vec[7:8, :]
            grad = (
                s - jnp.mean(s, axis=1, keepdims=True) - xhat * jnp.mean(s * xhat, axis=1, keepdims=True)
            ) * inv
            mg[at, :] = grad
            mf[at, :] = grad.astype(BF)
            small[0, 7:8, :] += col_sum(g * xhat)
            small[0, 8:9, :] += col_sum(g)
            small[0, 6:7, :] += col_sum(grad)
            return carry

        lax.fori_loop(0, rows // RB, second_norm, 0)
        layer_copy = local(in_out.at[0], out_layer)
        layer_copy.start()
        merged_pair.start()

        def ffn_back(r, carry):
            t = lax.rem(mp + r, mp_size)
            for j in range(shard // TILE):
                at = pl.ds(j * TILE, TILE)
                up_grad = mm_nt(mf[:rows, :], wd[t, at, :]) * gps[t, :, at]
                upl2[:rows, at] = up_grad.astype(BF)
            for j in range(width // TILE):
                at = pl.ds(j * TILE, TILE)
                mg[:, at] += mm_nt(upl2[:rows, :], wu[t, at, :])
            return carry

        lax.fori_loop(0, mp_size, ffn_back, 0)

        def norm_back(i, carry):
            at = pl.ds(pl.multiple_of(i * RB, RB), RB)
            g = mg[at, :]
            xhat = hid[at, :]
            s = g * vec[4:5, :]
            inv = rstd[at, 0:1]
            grad = (
                s - jnp.mean(s, axis=1, keepdims=True) - xhat * jnp.mean(s * xhat, axis=1, keepdims=True)
            ) * inv
            acc[at, :] = grad
            hlow[at, :] = grad.astype(BF)
            small[0, 4:5, :] += col_sum(g * xhat)
            small[0, 5:6, :] += col_sum(g)
            small[0, 3:4, :] += col_sum(grad)
            return carry

        lax.fori_loop(0, rows // RB, norm_back, 0)
        for j in range(width // TILE):
            at = pl.ds(j * TILE, TILE)
            gv[:, at] = mm_nt(hlow[...], wo[at, :]).astype(BF)

        def back_state(p, carry):
            at = lanes(p)
            total = den[:, at]
            inv = 1.0 / jnp.maximum(total, 1.0)
            g = gv[:, at].astype(F32)
            numer = (g * inv).astype(BF)
            sums = mm(two_parts(g * num[:, at]), bb[...])
            den_grad = jnp.where(total > 1.0, -sums * inv, 0.0)
            ngr[:, at] = numer
            mg[:, at] = den_grad
            qc, qs = feats(rq, p, 0)
            full = mm_tn(numer, jnp.concatenate([qc, qs], axis=1))
            state[p] = compact_of(full)
            ssum[0:1, at] = col_sum(qc.astype(F32) * den_grad)
            ssum[1:2, at] = col_sum(qs.astype(F32) * den_grad)
            return carry

        ssum[...] = jnp.zeros_like(ssum)
        ahead.finish()
        lax.fori_loop(0, PAIRS, back_state, 0)
        behind.early()

        def weight_grad(index, left_t, right):
            def body(i, carry):
                at = rds(i * TILE, TILE, TILE)
                for j in range(width // TILE):
                    to = pl.ds(j * TILE, TILE)
                    part[rds(index * width + i * TILE, TILE, TILE), to] = mm(
                        left_t[at, :], right[:, to]
                    ).astype(BF)
                return carry

            lax.fori_loop(0, width // TILE, body, 0)


        def j_base(job, upto):
            base = 0
            for s in range(upto):
                base = base + bit(jobs[job][s]) * (width >> (s + 1))
            return base

        reds = [red0, red1, red2]

        def part_of(job):
            if job < 4:
                return part.at[pl.ds(job * width, width)]
            return (wu, wd)[job % 2].at[across((1, 3)[(job - 4) // 2])]

        def add_rows(ref, start, count, received):
            step = min(count, 96)

            def body(i, carry):
                at = rds(start + i * step, step)
                ref[at, :] = (
                    ref[at, :].astype(F32) + received[rds(i * step, step), :].astype(F32)
                ).astype(BF)
                return carry

            lax.fori_loop(0, count // step, body, 0)

        def scatter_job(job):
            ref = part_of(job)
            for s in range(nhalf):
                half = width >> (s + 1)
                b = jobs[job][s]
                away = j_base(job, s) + (1 - bit(b)) * half
                copy = remote(ref.at[rds(away, half)], reds[s].at[job], flip(b))
                copy.start()
                yield
                copy.wait()
                add_rows(ref, j_base(job, s + 1), half, reds[s].at[job])
            for e, b in enumerate(range(nhalf, nbits)):
                at = rds(j_base(job, nhalf), piece)
                copy = remote(ref.at[at], redx.at[job, e], flip(b))
                copy.start()
                copy.wait()
                add_rows(ref, j_base(job, nhalf), piece, redx.at[job, e])
            yield

        outs = [out_q, out_o, out_v, out_k, out_up, out_down]
        final_copies = []

        def gather_job(job):
            for s in range(nhalf - 1, -1, -1):
                at = rds(job * width + j_base(job, s + 1), width >> (s + 1))
                copy = remote(gsum.at[at], gsum.at[at], flip(jobs[job][s]))
                copy.start()
                yield
                copy.wait()
            out = local(gsum.at[pl.ds(job * width, width)], outs[job])
            out.start()
            final_copies.append(out)
            yield

        quarter = piece // 2

        def quarter_row(first, t):
            which = lax.div(t, 2)
            base = (1 - which) * j_base(first, nhalf) + which * j_base(first + 1, nhalf)
            return (first + which) * width + base + lax.rem(t, 2) * quarter

        def z_job(first, slot):
            copies = []
            for i in range(1, mp_size):
                copies.append(
                    remote(
                        part.at[rds(quarter_row(first, across(i)), quarter)],
                        zr.at[slot, i - 1], {"mp": across(i)},
                    )
                )
                copies[-1].start()
            yield
            for copy in copies:
                copy.wait()
            at = rds(quarter_row(first, mp), quarter)
            total = part[at, :].astype(F32)
            for i in range(mp_size - 1):
                total = total + zr[slot, i].astype(F32)
            gsum[at, :] = total.astype(BF)
            copies = [remote(gsum.at[at], gsum.at[at], {"mp": across(i)}) for i in range(1, mp_size)]
            for copy in copies:
                copy.start()
            yield
            for copy in copies:
                copy.wait()
            yield

        def small_job():
            for b in range(nbits):
                copy = remote(small.at[b], smallr.at[b], flip(b))
                copy.start()
                yield
                copy.wait()
                small[b + 1] = small[b] + smallr[b]
            smallz[mp] = small[nbits]
            copies = [remote(smallz.at[mp], smallz.at[mp], {"mp": across(i)}) for i in range(1, mp_size)]
            for copy in copies:
                copy.start()
            yield
            for copy in copies:
                copy.wait()
            total = smallz[0]
            for z in range(1, mp_size):
                total = total + smallz[z]
            smallr[0, 0:8] = total[0:8]
            smallr[0, 8:16] = total[8:16]
            smallr[0, 15:16] = smallz[mp, 15:16] + smallz[across(2), 14:15]
            out = local(smallr.at[0], out_small)
            out.start()
            final_copies.append(out)
            yield

        def ff_z_job():
            copies = []
            for slot, job in enumerate((UB, DB)):
                at = rds(j_base(job, nhalf), piece)
                copies.append(remote(part_of(job).at[at], zf.at[slot], {"mp": across(2)}))
                copies[-1].start()
            yield
            for copy in copies:
                copy.wait()
            for slot, job in enumerate((UA, DA)):
                total = part_of(job)[rds(j_base(job, nhalf), piece), :].astype(F32) + zf[slot].astype(F32)
                gsum[rds(job * width + j_base(job, nhalf), piece), :] = total.astype(BF)
            yield

        Q, O, V, K, UA, DA, UB, DB = range(8)
        ff_z = ff_z_job()
        scatter = [scatter_job(job) for job in range(8)]
        gather = [gather_job(job) for job in range(6)]
        z_first = z_job(Q, 0)
        z_second = z_job(V, 1)
        smalls = small_job()

        def step(*generators):
            for g in generators:
                assert next(g, 1) is None

        tokt[...] = ctx[...].T
        weight_grad(O, tokt, hlow)
        step(scatter[O])

        def back_local(p, carry):
            at = lanes(p)
            qp = rq[:, at]
            kp = rk[:, at]
            vp = vv[:, at]
            numer = ngr[:, at]
            den_grad = mg[:, at]
            k2 = halves(kp)
            q2 = halves(qp)
            n2 = halves(numer)
            dh = den_grad.astype(BF)
            dl = (den_grad - dh.astype(F32)).astype(BF)
            x = dh * masks[2, :1] + dl * masks[3, :1]
            ds = (
                mm_nt(
                    jnp.concatenate([numer, x], axis=1),
                    jnp.concatenate([halves(vp), c1[...]], axis=1),
                )
                * m2[...]
            ).astype(BF)
            grad_q = mm(ds, k2)
            at_scores = (mm_nt(kp, q2) * mt2[...]).astype(BF)
            gv_part = mm(at_scores, n2)
            dst = (
                mm_nt(
                    jnp.concatenate([vp, ec[...]], axis=1),
                    jnp.concatenate([n2, halves(x)], axis=1),
                )
                * mt2[...]
            ).astype(BF)
            gk_part = mm(dst, q2)
            t = mm(numer, expand(state_in[p]))
            cq = cols[0]
            sq = cols[1]
            grad_q = grad_q + cq * t[:, :PAIR] + sq * t[:, PAIR:]
            grad_q = grad_q + den_grad * (cq * ssum_in[0:1, at] + sq * ssum_in[1:2, at])
            grad_q = jnp.where(qp.astype(F32) > 0.0, grad_q, 0.0)
            small[0, 0:1, at] = col_sum(grad_q)
            gq[:, at] = grad_q.astype(BF)
            normed[:, at] = gk_part
            hid[:, at] = gv_part
            return carry

        for c in range(CH):
            lax.fori_loop(c * PC, (c + 1) * PC, back_local, 0, unroll=True)
            if c == 0:
                step(scatter[O])
            behind.slot(c)
        behind.slot(3)
        behind.slot(4)
        tokt[...] = tok[...].T
        weight_grad(Q, tokt, gq)
        step(scatter[Q])

        def back_remote(p, carry):
            at = lanes(p)
            full = expand(grad_in[p])
            t = mm(vv[:, at], full)
            kc, ks = feats(rk, p, 2)
            ck = cols[2]
            sk = cols[3]
            grad_k = normed[:, at] + ck * (t[:, :PAIR] + gsum_in[0:1, at]) + sk * (
                t[:, PAIR:] + gsum_in[1:2, at]
            )
            grad_k = jnp.where(rk[:, at].astype(F32) > 0.0, grad_k, 0.0)
            small[0, 1:2, at] = col_sum(grad_k)
            gk[:, at] = grad_k.astype(BF)
            grad_v = hid[:, at] + mm_nt(jnp.concatenate([kc, ks], axis=1), full)
            small[0, 2:3, at] = col_sum(grad_v)
            gv[:, at] = grad_v.astype(BF)
            return carry

        lax.fori_loop(0, PAIRS, back_remote, 0)
        weight_grad(K, tokt, gk)
        step(scatter[K])
        weight_grad(V, tokt, gv)
        step(scatter[V], scatter[Q], scatter[O], scatter[K])

        for j in range(width // TILE):
            at = pl.ds(j * TILE, TILE)
            total = acc[:, at] + mm_nt(gq[...], wq[at, :]) + mm_nt(gk[...], wk[at, :])
            in_out[1, :, at] = (total + mm_nt(gv[...], wv[at, :])).astype(BF)
        input_copy = local(in_out.at[1], out_input)
        input_copy.start()
        step(scatter[V], scatter[Q], scatter[O])

        norm_pair.wait()
        merged_pair.wait()

        def shard_grads(t, up_job, down_job, row):
            for j in range(shard // TILE):
                at = pl.ds(j * TILE, TILE)
                u = mm(nf[...], wu[t, :, at]) + ub[t, 0:1, at]
                value, slope = gelu_both(u)
                up_grad = mm_nt(mf[...], wd[t, at, :]) * slope
                small[0, row : row + 1, at] = col_sum(up_grad)
                act2[:, at] = value.astype(BF)
                upl2[:, at] = up_grad.astype(BF)
            for j in range(width // TILE):
                at = pl.ds(j * TILE, TILE)
                part_of(up_job)[pl.ds(j * TILE, TILE), :] = mm_tn(nf[:, at], upl2[...]).astype(BF)
            for j in range(shard // TILE):
                at = pl.ds(j * TILE, TILE)
                part_of(down_job)[pl.ds(j * TILE, TILE), :] = mm_tn(act2[:, at], mf[...]).astype(BF)

        shard_grads(across(2), UB, DB, 14)
        step(scatter[UB], scatter[DB])
        step(scatter[Q])
        step(z_first, scatter[V], scatter[K])
        shard_grads(mp, UA, DA, 15)
        step(scatter[UA], scatter[DA], smalls)
        step(z_first)
        step(scatter[UB], scatter[DB])
        step(scatter[V], scatter[K], z_second)
        step(scatter[UA], scatter[DA], smalls)
        step(z_first, gather[Q], gather[O])
        step(scatter[UB], scatter[DB], z_second)
        step(scatter[UA], scatter[DA], smalls)
        step(gather[Q], gather[O])
        step(z_second, gather[V], gather[K])
        step(scatter[UB], scatter[DB], ff_z)
        step(gather[Q], gather[O], smalls)
        step(gather[V], gather[K])
        step(scatter[UA], scatter[DA], ff_z, gather[UA], gather[DA])
        step(gather[Q], gather[O])
        step(gather[V], gather[K], smalls)
        step(gather[UA], gather[DA])
        step(gather[V], gather[K])
        step(gather[UA], gather[DA])
        step(gather[UA], gather[DA])
        for _ in smalls:
            pass
        for g in scatter + gather + [z_first, z_second, ff_z, smalls] + list(weight_jobs.values()):
            assert next(g, 1) == 1
        behind.finish()
        layer_copy.wait()
        input_copy.wait()
        for copy in final_copies:
            copy.wait()

    def call(*operands):
        vm = pltpu.VMEM
        big = lambda *s: vm(s, BF)
        flt = lambda *s: vm(s, F32)
        nsem = 224
        square = jax.ShapeDtypeStruct((width, width), BF)
        scratch = [
            big(rows, width), big(rows, width), big(width, width), big(width, width), big(width, width),
            big(width, width), flt(16, width),
            big(mp_size, width, shard), big(mp_size, shard, width), flt(mp_size, 8, shard),
            big(rows, width), big(rows, width), big(rows, width),
            flt(rows, 2 * rows), flt(rows, 2 * rows), flt(4, rows, 128),
            big(2 * rows, PAIR), big(2 * PAIR, PAIR), big(2 * rows, PAIR), big(rows, PAIR), big(4, 16, PAIR),
            flt(PAIRS, HD, 2 * PAIR), big(PAIRS, HD, 2 * PAIR), flt(8, width), flt(8, width),
            big(PAIRS, HD, 2 * PAIR), flt(8, width), big(PAIRS, HD, 2 * PAIR), flt(8, width),
            flt(8, width),
            flt(rows, width), flt(rows, width), big(rows, width), flt(rows, width), flt(rows, 128),
            flt(rows, width), big(2 * rows, width), big(2 * rows, width),
            big(mp_size, rows, shard), flt(mp_size, rows, shard), big(2 * rows, shard), big(2 * rows, shard),
            big(2, piece, width), flt(rows, width), flt(rows, width),
            big(rows, width), big(rows, width),
            big(rows, width), big(rows, width), big(rows, width),
            big(4 * width, width), big(6 * width, width),
            big(8, width // 2, width), big(8, width // 4, width), big(8, width // 8, width),
            big(8, max(1, nbits - nhalf), 16 if nbits == nhalf else piece, width), big(2, mp_size - 1, piece // 2, width),
            flt(nbits + 1, 16, width), flt(nbits, 16, width), flt(mp_size, 16, width),
            big(width, rows), big(2, rows, width),
            pltpu.SemaphoreType.DMA((32,)), pltpu.SemaphoreType.DMA((nsem,)), pltpu.SemaphoreType.DMA((nsem,)),
        ]
        spec = pl.BlockSpec(memory_space=pltpu.VMEM)
        anywhere = pl.BlockSpec(memory_space=pl.ANY)
        return pl.pallas_call(
            kernel,
            out_shape=(
                jax.ShapeDtypeStruct((rows, width), BF),
                jax.ShapeDtypeStruct((rows, width), BF),
                square, square, square, square, square, square,
                jax.ShapeDtypeStruct((16, width), F32),
            ),
            in_specs=[pl.BlockSpec(memory_space=pltpu.SMEM)] + [spec] * 10 + [anywhere] * 8,
            out_specs=(anywhere,) * 9,
            scratch_shapes=scratch,
            compiler_params=pltpu.CompilerParams(
                collective_id=0, has_side_effects=True, vmem_limit_bytes=63 * 1024 * 1024
            ),
        )(*operands)

    return call


def widen(layer, back, grads, small):
    rows, width = layer.shape
    steps = 2

    def kernel(*refs):
        n = len(grads)
        ins, outs = refs[: n + 3], refs[n + 3 :]
        outs[0][...] = ins[0][...]
        outs[1][...] = ins[1][...]
        for g in range(n):
            outs[2 + g][...] = ins[2 + g][...].astype(F32)

        @pl.when(pl.program_id(0) == 0)
        def _():
            for row, out in zip((0, 1, 2, 3, 4, 5, 15, 6, 7, 8), outs[2 + n :]):
                out[...] = ins[2 + n][row : row + 1, :].reshape(width)

    block = lambda x: pl.BlockSpec((x.shape[0] // steps, x.shape[1]), lambda i: (i, 0))
    whole = pl.BlockSpec(small.shape, lambda i: (0, 0))
    vector = pl.BlockSpec((width,), lambda i: (0,))
    mats = [layer, back, *grads]
    return pl.pallas_call(
        kernel,
        grid=(steps,),
        in_specs=[block(x) for x in mats] + [whole],
        out_specs=[block(x) for x in mats] + [vector] * 10,
        out_shape=[jax.ShapeDtypeStruct(x.shape, BF) for x in (layer, back)]
        + [jax.ShapeDtypeStruct(x.shape, F32) for x in grads]
        + [jax.ShapeDtypeStruct((width,), F32)] * 10,
        compiler_params=pltpu.CompilerParams(vmem_limit_bytes=62 * 1024 * 1024),
    )(*mats, small)


def solution(mesh):
    dp_size, mp_size = mesh.shape["dp"], mesh.shape["mp"]

    def on_device(
        tokens, doc_starts, query_proj, key_proj, value_proj, query_bias, key_bias, value_bias,
        output_proj, output_bias, attn_gain, attn_shift, up_proj, up_bias, down_proj, down_bias,
        ffn_gain, ffn_shift, cotangent,
    ):
        _, rows, width = tokens.shape
        shard = up_proj.shape[1]
        call = build(dp_size, mp_size, rows, width, shard)
        layer_out, input_grad, gq, gk, gv, go, gu, gd, small = call(
            doc_starts, query_bias, key_bias, value_bias, output_bias, attn_gain, attn_shift,
            down_bias, ffn_gain, ffn_shift, up_bias, tokens[0], cotangent[0],
            query_proj, key_proj, value_proj, output_proj, up_proj, down_proj,
        )
        layer_out, input_grad, gq, gk, gv, go, gu, gd, *vecs = widen(
            layer_out, input_grad, (gq, gk, gv, go, gu, gd), small
        )
        bq, bk, bv, bo, ga, sa, bu, bd, gf, sf = vecs
        return (
            layer_out[None], input_grad[None], gq, gk, gv, bq, bk, bv, go, bo, ga, sa,
            gu, bu, gd, bd, gf, sf,
        )

    rows_spec = P("dp", "mp", None)
    placed = (
        rows_spec, P("dp", None), P(), P(), P(), P(), P(), P(), P(), P(), P(), P(),
        P(None, "mp"), P("mp"), P("mp", None), P(), P(), P(), rows_spec,
    )
    results = (
        rows_spec, rows_spec, P(), P(), P(), P(), P(), P(), P(), P(), P(), P(),
        P(None, "mp"), P("mp"), P("mp", None), P(), P(), P(),
    )
    return jax.shard_map(
        on_device, mesh=mesh, in_specs=placed, out_specs=results, check_vma=False
    )
```
